256 devices in a mesh: replica: 4 (over z_lo), shard: 64 (over y, x, z_hi, core).
Axes of the slice: x: 4, y: 4, z: 8 (z_hi: 2, z_lo: 4; z = z_hi * 4 + z_lo), core: 2. Of those that a mesh axis runs over, the one named last changes fastest.
Arguments:
- hidden: bfloat16 [2, 49152, 7168], P(None, ('replica', 'shard')), may hold values from -6 to 6
- norm_gains: bfloat16 [2, 7168], P(None, 'shard'), may hold values from 0.5 to 1.5
- head_block: bfloat16 [256, 7168], P('shard'), may hold values from -0.21875 to 0.21875
- targets: int32 [2, 49152], P(None, ('replica', 'shard')), may hold values from 0 to 511
- rest_lse: float32 [2, 49152], P(None, ('replica', 'shard')), may hold values from 8 to 12
- cotangent: float32 [2, 49152], P(None, ('replica', 'shard')), may hold values from 0.5 to 5
Outputs:
- grad_hidden: bfloat16 [2, 49152, 7168], P(None, ('replica', 'shard'))
- grad_head: float32 [256, 7168], P('shard')
- grad_gains: float32 [2, 7168], P(None, 'shard')
The draws below stay inside these ranges and needn't reach their ends.
All inputs are finite; a program needn't handle non-finite values.
Results may differ from the reference program's by a relative error of at most 0.0063.
Values may be sent and summed in bfloat16 or wider, within the bound.
A program may use at most 128 MiB of HBM per device.

```python
import math
import jax
import jax.numpy as jnp
from jax import lax

D = 7168
VCH = 256
TOK_DEV = 192
TOKENS = 49152


def place_ends(drawn, rng, smallest, top_value):
    spot = [jax.random.randint(jax.random.fold_in(rng, axis), (), 0, length) for axis, length in enumerate(drawn.shape)]
    longest = drawn.shape.index(max(drawn.shape))
    beside = spot[:longest] + [(spot[longest] + 1) % drawn.shape[longest]] + spot[longest + 1:]
    return drawn.at[tuple(spot)].set(smallest).at[tuple(beside)].set(top_value)


def block_levels(own_key, extent, split, least, top_value):
    def one(position, shards_of):
        draws = jax.random.uniform(jax.random.fold_in(jax.random.fold_in(own_key, 6), position), (shards_of,), jnp.float32, least / len(split), top_value / len(split))
        return jnp.repeat(jnp.exp(draws), extent[position] // shards_of).reshape((-1,) + (1,) * (len(extent) - position - 1))

    level = one(*split[0])
    for cut in split[1:]:
        level = level * one(*cut)
    return level


def centred(own_key, extent, spread, most, split=(), kind=jnp.bfloat16):
    loudness = block_levels(own_key, extent, split, -0.22, 0.18) if split else 1.0
    entries = jax.random.normal(own_key, extent, jnp.float32) * spread * loudness
    return jnp.minimum(jnp.maximum(entries, -most), most).astype(kind)


def setup_inputs(seed: int = 0) -> dict:
    arg_keys = jax.random.split(jax.random.key(seed), 7)
    return {
        "hidden": centred(arg_keys[0], (2, TOKENS, D), 1.0, 6.0, ((1, 256),)),
        "norm_gains": jnp.clip(1.0 + 0.1 * jax.random.normal(arg_keys[1], (2, D), jnp.float32), 0.5, 1.5).astype(jnp.bfloat16),
        "head_block": centred(arg_keys[2], (VCH, D), (D // 9) ** -0.5, 0.21875, ((0, 64),)),
        "targets": place_ends(jax.random.randint(arg_keys[3], (2, TOKENS), 0, 2 * VCH), jax.random.fold_in(arg_keys[3], 1), 0, (2 * VCH) - 1).astype(jnp.int32),
        "rest_lse": jnp.clip(8.0 + 4.0 * jax.random.uniform(arg_keys[4], (2, TOKENS), jnp.float32) ** block_levels(arg_keys[4], (2, TOKENS), ((1, 256),), -0.2, 0.2), 8.0, 12.0),
        "cotangent": jnp.clip(jnp.exp(math.log(5.0) - 2.3025851 * jax.random.uniform(arg_keys[5], (2, TOKENS), jnp.float32) ** block_levels(arg_keys[5], (2, TOKENS), ((1, 256),), -0.2, 0.2)), 0.5, 5.0),
    }


eps = 1e-06

def head_pass(block_hidden, gains, head, block_targets, block_rest, block_cot):
    xf = block_hidden.astype(jnp.float32)
    scale = lax.rsqrt(lax.optimization_barrier(jnp.mean(xf * xf, axis=-1)) + eps)
    gainf = gains.astype(jnp.float32)
    normed = (xf * scale[..., None] * gainf[:, None, :]).astype(jnp.bfloat16)
    rows = normed.shape[0] * normed.shape[1]
    flat = normed.reshape(rows, normed.shape[2])
    logits = lax.dot_general(flat, head, (((1,), (1,)), ((), ())), preferred_element_type=jnp.float32)
    total = jnp.log(jnp.exp(block_rest.reshape(rows)) + lax.optimization_barrier(jnp.sum(jnp.exp(logits), axis=-1)))
    column = jnp.arange(head.shape[0], dtype=jnp.int32)
    onehot = (block_targets.reshape(rows)[:, None] == column[None, :]).astype(jnp.float32)
    dlogits = (block_cot.reshape(rows)[:, None] * (jnp.exp(logits - total[:, None]) - onehot)).astype(jnp.bfloat16)
    dnormed = jnp.dot(dlogits, head, preferred_element_type=jnp.float32).reshape(xf.shape)
    inner = lax.optimization_barrier(jnp.mean(xf * gainf[:, None, :] * dnormed, axis=-1))
    grad_x = scale[..., None] * gainf[:, None, :] * dnormed - xf * (scale ** 3 * inner)[..., None]
    grad_w = lax.dot_general(dlogits, flat, (((0,), (0,)), ((), ())), preferred_element_type=jnp.float32)
    grad_g = lax.optimization_barrier(jnp.sum(dnormed * xf * scale[..., None], axis=1))
    return (grad_x.astype(jnp.bfloat16), grad_w, grad_g)

def reference(hidden, norm_gains, head_block, targets, rest_lse, cotangent):
    width = TOK_DEV
    count = hidden.shape[1] // width

    def step(carry, index):
        start = (index * width).astype(jnp.int32)
        block_hidden = lax.dynamic_slice_in_dim(hidden, start, width, 1)
        block_targets = lax.dynamic_slice_in_dim(targets, start, width, 1)
        block_rest = lax.dynamic_slice_in_dim(rest_lse, start, width, 1)
        block_cot = lax.dynamic_slice_in_dim(cotangent, start, width, 1)
        grad_x, grad_w, grad_g = head_pass(block_hidden, norm_gains, head_block, block_targets, block_rest, block_cot)
        return ((carry[0] + grad_w, carry[1] + grad_g), grad_x)
    init = (jnp.zeros(head_block.shape, jnp.float32), jnp.zeros(norm_gains.shape, jnp.float32))
    sums, blocks = lax.scan(step, init, jnp.arange(count, dtype=jnp.int32))
    grad_hidden = jnp.transpose(blocks, (1, 0, 2, 3)).reshape(hidden.shape)
    return (grad_hidden, sums[0], sums[1])
```

```python
import jax
import jax.numpy as jnp
from jax import lax
from jax.experimental import pallas as pl
from jax.experimental.pallas import tpu as pltpu
from jax.sharding import PartitionSpec as P

eps = 1e-06
F32, BF16, I32 = jnp.float32, jnp.bfloat16, jnp.int32
MESH = pl.DeviceIdType.MESH

D = 7168
HALF = D // 2
G = 896
W = 2 * G
V = 256
T = 384
RT = 32
NRT = T // RT
GN = 112
NSEM = 160


def iota(shape, dim):
    return lax.broadcasted_iota(I32, shape, dim)


def kernel(
    hid_ref, gain_ref, head_ref, tgt_ref, rest_ref, cot_ref,
    gx_ref, gw_ref, gg_ref,
    xv, nv, hv, r_own, r_sib, raw, gcol, gblk, gfull, scale_v,
    dl_t, dl_v, coef_v, dn_v, gacc, p_scr, xs, xr, s0, s1, f0, f1, n0, n1,
    t0, t1, fb0, fb1, nb0, nb1, zsum, zp, zr, yv, fr,
    local_sem, send_sem, recv_sem, zsend_sem, zrecv_sem, fsend_sem, frecv_sem,
):
    zl = lax.axis_index("replica")
    shard = lax.axis_index("shard")
    c = shard & 1
    zh = (shard >> 1) & 1
    x = (shard >> 2) & 3
    y = shard >> 4
    z = zh * 4 + zl
    pc = x + c * (y - x)
    qc = y + c * (x - y)

    def device(q, p, zz, cc):
        xx = p + c * (q - p)
        yy = q + c * (p - q)
        return (zz & 3, ((yy * 4 + xx) * 2 + (zz >> 2)) * 2 + cc)

    def at(dq=0, dp=0):
        return device((qc + dq) & 3, (pc + dp) & 3, z, c)

    sibling = (zl, shard + 1 - 2 * c)

    count = [0]
    started = []

    def send(src, dst, target, start=True):
        i = count[0]
        count[0] += 1
        copy = pltpu.make_async_remote_copy(
            src_ref=src, dst_ref=dst, send_sem=send_sem.at[i], recv_sem=recv_sem.at[i],
            device_id=target, device_id_type=MESH,
        )
        if start:
            copy.start()
            started.append(copy)
        return copy

    loads = []
    for i in range(4):
        rows = pl.ds(i * 96, 96)
        copy = pltpu.make_async_copy(hid_ref.at[rows], xv.at[rows], local_sem.at[i])
        copy.start()
        loads.append(copy)

    partners = [sibling]
    for d in (1, 2, 3):
        partners += [at(dq=d), at(dp=d)]
    for d in range(1, 8):
        partners.append(device(qc, pc, (z + d) & 7, c))
    for d in range(1, 4):
        partners.append(device(qc, pc, zh * 4 + ((zl + d) & 3), 1 - c))
    barrier = pltpu.get_barrier_semaphore()
    for partner in partners:
        pl.semaphore_signal(barrier, inc=1, device_id=partner, device_id_type=MESH)

    hb = head_ref[...].astype(F32)
    for h in range(2):
        parts = [hb[:, (h * 4 + f) * G:(h * 4 + f + 1) * G] for f in range(4)]
        raw[h] = jnp.concatenate(parts, axis=0).astype(BF16)
    r_own[qc, pc, zh, c] = raw[c]
    gpad = jnp.concatenate([gain_ref[...].astype(F32), jnp.zeros((2, 128 - GN), F32)], axis=1)
    gcol[zh * 2 + c] = jnp.concatenate([gpad, jnp.zeros((6, 128), F32)], axis=0)

    pl.semaphore_wait(barrier, len(partners))

    w = zh * 2 + c
    m_g = send(gcol.at[w], gcol.at[w], sibling)
    m_h = send(raw.at[1 - c], r_own.at[pc, qc, zh, c], sibling)
    edge = (zl == 0) | (zl == 3)
    step = jnp.where(zl == 3, 1, -1)
    m_g.wait_recv()
    z_gain = [
        send(gcol.at[pl.ds(zh * 2, 2)], gcol.at[pl.ds(zh * 2, 2)],
             device(qc, pc, (z + d * step) & 7, c), start=False)
        for d in (1, 2)
    ]

    @pl.when(edge)
    def _():
        for copy in z_gain:
            copy.start()

    m_h.wait_recv()

    def block(q, p, k):
        return r_own.at[q & 3, p & 3, k]

    own = {}

    def spread(k, name, q, p, piece=None):
        ref = block(q, p, k)
        own[name, "q+"] = send(ref, ref, at(dq=1))
        own[name, "q-"] = send(ref, ref, at(dq=-1))

    def begin(k, n):
        ref = block(qc, pc, k)
        own[n, "p+"] = send(ref, ref, at(dp=1))
        own[n, "p-"] = send(ref, ref, at(dp=-1))
        spread(k, (n, 0), qc, pc)

    def p_near(k, n):
        own[n, "p+"].wait_recv()
        ref = block(qc, pc - 1, k).at[0]
        own[n, "pf+"] = send(ref, ref, at(dp=1))
        spread(k, (n, -1), qc, pc - 1)
        own[n, "p-"].wait_recv()
        ref = block(qc, pc + 1, k).at[1]
        own[n, "pf-"] = send(ref, ref, at(dp=-1))
        spread(k, (n, 1), qc, pc + 1)

    def p_far(k, n):
        own[n, "pf+"].wait_recv()
        own[n, "pf-"].wait_recv()
        spread(k, (n, 2), qc, pc + 2)

    def to_sibling(k, n, q):
        ref = r_own.at[q & 3, :, k]
        own[n, "sib", count[0]] = copy = send(ref, r_sib.at[q & 3, :, k], sibling)
        return copy

    def q_forward(k, n, b):
        own[(n, b), "q+"].wait_recv()
        ref = block(qc - 1, pc + b, k).at[0]
        own[(n, b), "qf+"] = send(ref, ref, at(dq=1))
        own[(n, b), "q-"].wait_recv()
        ref = block(qc + 1, pc + b, k).at[1]
        own[(n, b), "qf-"] = send(ref, ref, at(dq=-1))

    def q_far(k, n):
        for b in (0, -1, 1, 2):
            own[(n, b), "qf+"].wait_recv()
            own[(n, b), "qf-"].wait_recv()

    def scale_tiles(first, last):
        def body(i, carry):
            rows = pl.ds(pl.multiple_of(i * RT, RT), RT)
            total = jnp.zeros((RT, 128), F32)
            for j in range(D // G):
                part = xv[rows, j * G:(j + 1) * G].astype(F32)
                part = part * part
                for l in range(G // 128):
                    total += part[:, l * 128:(l + 1) * 128]
            mean = jnp.sum(total, axis=1, keepdims=True) * (1.0 / D)
            scale_v[rows] = jnp.broadcast_to(lax.rsqrt(mean + eps), (RT, 128))
            return carry
        lax.fori_loop(first, last, body, 0)

    def lanes(v):
        return jnp.concatenate([v] * (G // 128), axis=1)

    def normed_tiles(first, last):
        def body(i, carry):
            rows = pl.ds(pl.multiple_of(i * RT, RT), RT)
            k = jnp.where(i >= NRT // 2, 1, 0)
            s = lanes(scale_v[rows])
            for j in range(D // G):
                cols = slice(j * G, (j + 1) * G)
                g = gfull[k, :, cols]
                g = jnp.concatenate([g] * (RT // 8), axis=0)
                nv[rows, cols] = (xv[rows, cols].astype(F32) * s * g).astype(BF16)
            return carry
        lax.fori_loop(first, last, body, 0)

    def pieces(rows, shift):
        r = iota((rows, G), 0)
        p = (r >> shift) & 3
        q = r >> (shift + 2)
        return r, p + c * (q - p), q + c * (p - q)

    def spread_matrix():
        j = iota((128, G), 0)
        col = iota((128, G), 1)
        hit = jnp.zeros((128, G), jnp.bool_)
        for m in range(8):
            hit = hit | (col == j + GN * m)
        return jnp.where(hit & (j < GN), 1.0, 0.0).astype(BF16)

    def inside(rows, shift, w_of):
        r, xx, _ = pieces(rows, shift)
        m = (xx & 1) * 4 + w_of(r)
        col = iota((rows, G), 1)
        return (col >= m * GN) & (col < (m + 1) * GN)

    def make_gains():
        lhs = gblk[...].reshape(128, 128).astype(BF16)
        u = jnp.dot(lhs, spread_matrix(), preferred_element_type=F32)
        u = jnp.where(inside(128, 3, lambda r: (r >> 1) & 3), u, 0.0).astype(BF16)
        o = iota((16, 128), 0)
        i = iota((16, 128), 1)
        p = (i >> 3) & 3
        q = i >> 5
        xx = p + c * (q - p)
        yy = q + c * (p - q)
        sel = ((yy * 2 + (xx >> 1)) == (o >> 1)) & ((i & 1) == (o & 1))
        full = jnp.dot(jnp.where(sel, 1.0, 0.0).astype(BF16), u, preferred_element_type=F32)
        for j in range(8):
            for k in range(2):
                row = full[2 * j + k:2 * j + k + 1]
                gfull[k, :, j * G:(j + 1) * G] = jnp.broadcast_to(row, (8, G))

    def permutation():
        o = iota((V, V), 0)
        i = iota((V, V), 1)
        src = ((o >> 4) & 3) * 64 + ((o >> 2) & 3) * 16 + (o >> 6) * 4 + (o & 3)
        return jnp.where(i == src, 1.0, 0.0).astype(BF16)

    def place(buf, half, core, q):
        q = q & 3
        rows = jnp.dot(permutation(), buf[q].reshape(V, G), preferred_element_type=F32).astype(BF16)
        for f in range(4):
            cols = pl.ds(pl.multiple_of(half * HALF + f * G, 128), G)
            for p in range(4):
                yy = q + core * (p - q)
                xx = p + core * (q - p)
                hv[yy * 4 + xx, :, cols] = rows[f * 64 + p * 16:f * 64 + (p + 1) * 16]

    begin(zh, 0)
    z_head = [
        send(block(qc, pc, zh), block(qc, pc, zh), device(qc, pc, (z + d * step) & 7, c), start=False)
        for d in (1, 2)
    ]

    @pl.when(edge)
    def _():
        for copy in z_head:
            copy.start()

    def z_arrives(copies):
        @pl.when(edge)
        def _():
            copies[0].wait_recv()

        @pl.when(jnp.logical_not(edge))
        def _():
            copies[1].wait_recv()

    z_arrives(z_gain)
    gblk[qc, pc] = jnp.concatenate([gcol[i][0:2] for i in range(4)], axis=0)
    g_p = [send(gblk.at[qc, pc], gblk.at[qc, pc], at(dp=d)) for d in (1, -1, 2)]
    for copy in loads:
        copy.wait()
    scale_tiles(0, 3)
    p_near(zh, 0)
    z_arrives(z_head)
    begin(1 - zh, 1)
    for copy in g_p:
        copy.wait_recv()
    g_q = [send(gblk.at[qc], gblk.at[qc], at(dq=d)) for d in (1, -1, 2)]
    scale_tiles(3, 6)
    p_far(zh, 0)
    q_forward(zh, 0, 0)
    scale_tiles(6, 9)
    p_near(1 - zh, 1)
    q_forward(zh, 0, -1)
    q_forward(zh, 0, 1)
    scale_tiles(9, 12)
    p_far(1 - zh, 1)
    to_sibling(zh, 0, qc)
    for copy in g_q:
        copy.wait_recv()
    make_gains()
    q_forward(zh, 0, 2)
    q_forward(1 - zh, 1, 0)
    sib = [to_sibling(zh, 0, qc + 1), to_sibling(zh, 0, qc - 1), to_sibling(1 - zh, 1, qc)]
    normed_tiles(0, 6)
    q_forward(1 - zh, 1, -1)
    q_forward(1 - zh, 1, 1)
    q_far(zh, 0)
    to_sibling(zh, 0, qc + 2)
    q_forward(1 - zh, 1, 2)
    to_sibling(1 - zh, 1, qc + 1)
    to_sibling(1 - zh, 1, qc - 1)
    normed_tiles(6, 12)
    place(r_own, c, c, qc)
    place(r_own, c, c, qc + 1)
    place(r_own, c, c, qc - 1)
    q_far(1 - zh, 1)
    to_sibling(1 - zh, 1, qc + 2)
    place(r_own, c, c, qc + 2)

    def logits_part(half):
        total = None
        for j in range(2):
            cols = pl.ds(pl.multiple_of(half * HALF + j * W, 128), W)
            part = lax.dot_general(
                hv[:, :, cols].reshape(V, W), nv[:, cols],
                (((1,), (1,)), ((), ())), preferred_element_type=F32)
            total = part if total is None else total + part
        return total

    first_half = logits_part(c)
    for key in list(own):
        if key[1] == "sib":
            own[key].wait_recv()
    for q in range(4):
        place(r_sib, 1 - c, 1 - c, q)
    logits = first_half + logits_part(1 - c)

    def row(ref):
        return jnp.concatenate([ref[0:1], ref[1:2]], axis=1)

    total = jnp.log(jnp.exp(row(rest_ref)) + jnp.sum(jnp.exp(logits), axis=0, keepdims=True))
    onehot = jnp.where(row(tgt_ref) == iota((V, T), 0), 1.0, 0.0)
    grad = (row(cot_ref) * (jnp.exp(logits - total) - onehot)).astype(BF16)
    dl_t[...] = grad
    grad = grad.astype(F32)
    inner = jnp.sum(grad * logits, axis=0, keepdims=True) * (1.0 / D)

    def partial(half, j):
        for i in range(2):
            cols = pl.ds(pl.multiple_of(half * HALF + j * W + i * G, 128), G)
            p_scr[:, :, i * G:(i + 1) * G] = jnp.dot(
                dl_t[...], nv[:, cols], preferred_element_type=F32).reshape(16, 16, G)

    def give(j):
        partial(1 - c, j)

        def body(b, carry):
            xs[j, b] = p_scr[b].astype(BF16)
            return carry
        lax.fori_loop(0, 16, body, 0)
        return send(xs.at[j], xr.at[j], sibling)

    def take(j, copy, s):
        copy.wait_recv()

        def body(b, carry):
            q, p = b >> 2, b & 3
            yy = q + c * (p - q)
            xx = p + c * (q - p)
            both = p_scr[yy * 4 + xx] + xr[j, yy * 4 + xx].astype(F32)
            s[q, p, :, 0:W] = both.astype(BF16)
            return carry
        lax.fori_loop(0, 16, body, 0)

    def ring_begin(s, width, f, n, hop, here, rows_of):
        lo, hi = slice(0, G), slice(G, width)
        far, up, down = (here + 2) & 3, (here + 1) & 3, (here - 1) & 3
        m = {}
        m["f+"] = send(rows_of(s, far, lo), f[0], hop(1))
        m["f-"] = send(rows_of(s, far, hi), f[1], hop(-1))
        m["n+"] = send(rows_of(s, up, hi), rows_of(n, 0, hi), hop(1))
        m["n-"] = send(rows_of(s, down, lo), rows_of(n, 1, lo), hop(-1))
        return m

    def ring_join(m, s, width, f, n, hop, here, rows_of):
        lo, hi = slice(0, G), slice(G, width)
        up, down = (here + 1) & 3, (here - 1) & 3
        m["f+"].wait_recv()
        ref = rows_of(s, up, lo)
        ref[...] = (ref[...].astype(F32) + f[0][...].astype(F32)).astype(BF16)
        m["j+"] = send(ref, rows_of(n, 0, lo), hop(1))
        m["f-"].wait_recv()
        ref = rows_of(s, down, hi)
        ref[...] = (ref[...].astype(F32) + f[1][...].astype(F32)).astype(BF16)
        m["j-"] = send(ref, rows_of(n, 1, hi), hop(-1))

    def ring_end(m):
        for name in ("n+", "n-", "j+", "j-"):
            m[name].wait_recv()

    def slab(ref, i, cols):
        return ref.at[i, :, :, cols]

    def tile(ref, i, cols):
        return ref.at[i, :, cols]

    def hop_q(d):
        return at(dq=d)

    def hop_p(d):
        return at(dp=d)

    big = [(s0, W, (f0.at[0], f0.at[1]), n0), (s1, W + 128, (f1.at[0, :, :, 0:G], f1.at[1]), n1)]
    small = [(t0, W, (fb0.at[0], fb0.at[1]), nb0), (t1, W + 128, (fb1.at[0, :, 0:G], fb1.at[1]), nb1)]

    def big_end(j, m):
        ring_end(m)
        s, _, _, n = big[j]
        t = small[j][0]

        def body(p, carry):
            t[p] = (s[qc, p].astype(F32) + n[0, p].astype(F32) + n[1, p].astype(F32)).astype(BF16)
            return carry
        lax.fori_loop(0, 4, body, 0)

    def small_end(j, m):
        ring_end(m)
        t, width, _, n = small[j]
        zsum[:, 0:width] = t[pc].astype(F32) + n[0].astype(F32) + n[1].astype(F32)
        for owner in range(4):
            rows = slice(owner * 4, owner * 4 + 4)
            zp[j, owner, :, 0:G] = jnp.concatenate([zsum[rows, 0:G], zsum[rows, G:W]], axis=0)
            if j == 1:
                zp[j, owner, :, G:G + 128] = zsum[0:8, W:W + 128]
        for owner in range(4):
            target = (owner >> 1) * 4 + (owner & 1) * 2 + j
            copy = z_copy(j, owner)

            @pl.when(target != z)
            def _():
                copy.start()

            @pl.when(target == z)
            def _():
                zr[z, :, 0:G + 128 * j] = zp[j, owner, :, 0:G + 128 * j]

    def z_copy(j, owner):
        wide = G + 128 * j
        target = (owner >> 1) * 4 + (owner & 1) * 2 + j
        return pltpu.make_async_remote_copy(
            src_ref=zp.at[j, owner, :, 0:wide], dst_ref=zr.at[z, :, 0:wide],
            send_sem=zsend_sem.at[j, owner], recv_sem=zrecv_sem.at[z],
            device_id=device(qc, pc, target, c), device_id_type=MESH,
        )

    def f_copy(to):
        return pltpu.make_async_remote_copy(
            src_ref=yv, dst_ref=fr.at[c, zl & 1],
            send_sem=fsend_sem.at[to], recv_sem=frecv_sem.at[c * 2 + (zl & 1)],
            device_id=device(qc, pc, zh * 4 + to, zl >> 1), device_id_type=MESH,
        )

    def z_end(j):
        wide = G + 128 * j

        @pl.when((zl & 1) == j)
        def _():
            for src in range(8):
                @pl.when(src != z)
                def _():
                    pltpu.make_async_remote_copy(
                        src_ref=zp.at[j, 0, :, 0:wide], dst_ref=zr.at[src, :, 0:wide],
                        send_sem=zsend_sem.at[j, 0], recv_sem=zrecv_sem.at[src],
                        device_id=sibling, device_id_type=MESH,
                    ).wait_recv()
            total = zr[0, :, 0:wide]
            for src in range(1, 8):
                total = total + zr[src, :, 0:wide]
            yv[:, 0:wide] = total
            if j == 0:
                yv[:, G:G + 128] = jnp.zeros((8, 128), F32)
            for to in range(4):
                mine = (zl == to) & (c == (zl >> 1))

                @pl.when(jnp.logical_not(mine))
                def _():
                    f_copy(to).start()

                @pl.when(mine)
                def _():
                    fr[c, zl & 1] = yv[...]

    def hidden_block(j):
        cols = pl.ds(pl.multiple_of(j * G, 128), G)
        dn_v[...] = jnp.dot(dl_v[...], hv[:, :, cols].reshape(V, G), preferred_element_type=F32)
        for k in range(2):
            def body(i, acc):
                rows = pl.ds(pl.multiple_of(i * RT, RT), RT)
                s = lanes(scale_v[rows])
                g = jnp.concatenate([gfull[k, :, cols]] * (RT // 8), axis=0)
                xf = xv[rows, cols].astype(F32)
                dn = dn_v[rows]
                sdn = s * dn
                xv[rows, cols] = (g * sdn - xf * lanes(coef_v[rows])).astype(BF16)
                prod = sdn * xf
                for r in range(RT // 8):
                    acc = acc + prod[r * 8:(r + 1) * 8]
                return acc
            acc = lax.fori_loop(k * NRT // 2, (k + 1) * NRT // 2, body, jnp.zeros((8, G), F32))
            gacc[j * 2 + k] = acc

    outs = []

    def hidden_out(j):
        cols = pl.ds(pl.multiple_of(j * G, 128), G)
        copy = pltpu.make_async_copy(xv.at[:, cols], gx_ref.at[:, cols], local_sem.at[4 + j])
        copy.start()
        outs.append(copy)

    def rider():
        full = jnp.concatenate(
            [jnp.sum(gacc[i], axis=0, keepdims=True) for i in range(16)], axis=0).astype(BF16)
        o = iota((V, 16), 0)
        i = iota((V, 16), 1)
        p = (o >> 4) & 3
        q = o >> 6
        xx = p + c * (q - p)
        yy = q + c * (p - q)
        sel = ((yy * 2 + (xx >> 1)) == (i >> 1)) & ((o & 1) == (i & 1)) & ((o & 15) < 8)
        u = jnp.dot(jnp.where(sel, 1.0, 0.0).astype(BF16), full, preferred_element_type=F32)
        u = jnp.where(inside(V, 4, lambda r: (r >> 1) & 3), u, 0.0).astype(BF16)
        out = lax.dot_general(
            u, spread_matrix(), (((1,), (1,)), ((), ())), preferred_element_type=F32)
        s1[:, :, :, W:W + 128] = out.astype(BF16).reshape(4, 4, 16, 128)

    give0 = give(0)
    partial(c, 0)
    take(0, give0, s0)
    b0 = ring_begin(s0, W, big[0][2], n0, hop_q, qc, slab)
    dl_v[...] = jnp.transpose(dl_t[...].astype(F32)).astype(BF16)
    coef = jnp.transpose(jnp.broadcast_to(inner, (128, T)))
    sc = scale_v[...]
    coef_v[...] = coef * sc * sc
    for j in range(3):
        hidden_block(j)
        hidden_out(j)
    ring_join(b0, s0, W, big[0][2], n0, hop_q, qc, slab)
    give1 = give(1)
    for j in range(3, 8):
        hidden_block(j)
        hidden_out(j)
    rider()
    partial(c, 1)
    take(1, give1, s1)
    b1 = ring_begin(s1, W + 128, big[1][2], n1, hop_q, qc, slab)
    big_end(0, b0)
    c0 = ring_begin(t0, W, small[0][2], nb0, hop_p, pc, tile)
    ring_join(b1, s1, W + 128, big[1][2], n1, hop_q, qc, slab)
    ring_join(c0, t0, W, small[0][2], nb0, hop_p, pc, tile)
    small_end(0, c0)
    big_end(1, b1)
    c1 = ring_begin(t1, W + 128, small[1][2], nb1, hop_p, pc, tile)
    z_end(0)
    ring_join(c1, t1, W + 128, small[1][2], nb1, hop_p, pc, tile)
    small_end(1, c1)
    z_end(1)

    for src in range(2):
        for ch in range(2):
            mine = (c == src) & (zl == c * 2 + ch)

            @pl.when(jnp.logical_not(mine))
            def _():
                pltpu.make_async_remote_copy(
                    src_ref=yv, dst_ref=fr.at[src, ch],
                    send_sem=fsend_sem.at[0], recv_sem=frecv_sem.at[src * 2 + ch],
                    device_id=sibling, device_id_type=MESH,
                ).wait_recv()
            for sub in range(2):
                first = src * HALF + ch * W + sub * G
                gw_ref[:, first:first + G] = fr[src, ch, sub * 4:sub * 4 + 4, 0:G]
    gains = fr[0, 1, :, G:G + 128] + fr[1, 1, :, G:G + 128]
    mine = jnp.zeros((2, 128), F32)
    for i in range(4):
        mine = jnp.where(w == i, gains[i * 2:i * 2 + 2], mine)
    gg_ref[...] = mine[:, 0:GN]

    for copy in started:
        copy.wait_send()

    @pl.when(edge)
    def _():
        for copy in z_gain + z_head:
            copy.wait_send()
    for j in range(2):
        for owner in range(4):
            target = (owner >> 1) * 4 + (owner & 1) * 2 + j

            @pl.when(target != z)
            def _():
                z_copy(j, owner).wait_send()
    for to in range(4):
        @pl.when(jnp.logical_not((zl == to) & (c == (zl >> 1))))
        def _():
            f_copy(to).wait_send()
    for copy in outs:
        copy.wait()


def local(hidden, norm_gains, head_block, targets, rest_lse, cotangent):
    any_space = pl.BlockSpec(memory_space=pl.ANY)
    vmem = pl.BlockSpec(memory_space=pltpu.VMEM)
    scratch = [
        pltpu.VMEM((T, D), BF16),
        pltpu.VMEM((T, D), BF16),
        pltpu.VMEM((16, 16, D), BF16),
        pltpu.VMEM((4, 4, 2, 2, 16, G), BF16),
        pltpu.VMEM((4, 4, 2, 2, 16, G), BF16),
        pltpu.VMEM((2, 16, G), BF16),
        pltpu.VMEM((4, 8, 128), F32),
        pltpu.VMEM((4, 4, 8, 128), F32),
        pltpu.VMEM((2, 8, D), F32),
        pltpu.VMEM((T, 128), F32),
        pltpu.VMEM((V, T), BF16),
        pltpu.VMEM((T, V), BF16),
        pltpu.VMEM((T, 128), F32),
        pltpu.VMEM((T, G), F32),
        pltpu.VMEM((16, 8, G), F32),
        pltpu.VMEM((16, 16, W), F32),
        pltpu.VMEM((2, 16, 16, W), BF16),
        pltpu.VMEM((2, 16, 16, W), BF16),
        pltpu.VMEM((4, 4, 16, W), BF16),
        pltpu.VMEM((4, 4, 16, W + 128), BF16),
        pltpu.VMEM((2, 4, 16, G), BF16),
        pltpu.VMEM((2, 4, 16, G + 128), BF16),
        pltpu.VMEM((2, 4, 16, W), BF16),
        pltpu.VMEM((2, 4, 16, W + 128), BF16),
        pltpu.VMEM((4, 16, W), BF16),
        pltpu.VMEM((4, 16, W + 128), BF16),
        pltpu.VMEM((2, 16, G), BF16),
        pltpu.VMEM((2, 16, G + 128), BF16),
        pltpu.VMEM((2, 16, W), BF16),
        pltpu.VMEM((2, 16, W + 128), BF16),
        pltpu.VMEM((16, W + 128), F32),
        pltpu.VMEM((2, 4, 8, G + 128), F32),
        pltpu.VMEM((8, 8, G + 128), F32),
        pltpu.VMEM((8, G + 128), F32),
        pltpu.VMEM((2, 2, 8, G + 128), F32),
        pltpu.SemaphoreType.DMA((12,)),
        pltpu.SemaphoreType.DMA((NSEM,)),
        pltpu.SemaphoreType.DMA((NSEM,)),
        pltpu.SemaphoreType.DMA((2, 4)),
        pltpu.SemaphoreType.DMA((8,)),
        pltpu.SemaphoreType.DMA((4,)),
        pltpu.SemaphoreType.DMA((4,)),
    ]
    grad_hidden, grad_head, grad_gains = pl.pallas_call(
        kernel,
        out_shape=(
            jax.ShapeDtypeStruct((T, D), BF16),
            jax.ShapeDtypeStruct((4, D), F32),
            jax.ShapeDtypeStruct((2, GN), F32),
        ),
        in_specs=[any_space, vmem, vmem, vmem, vmem, vmem],
        out_specs=(any_space, vmem, vmem),
        scratch_shapes=scratch,
        compiler_params=pltpu.CompilerParams(
            collective_id=0, has_side_effects=True, vmem_limit_bytes=60 << 20),
        cost_estimate=pl.CostEstimate(
            flops=6 * T * D * V, bytes_accessed=4 * T * D, transcendentals=2 * T * V),
        name="head_backward",
    )(hidden.reshape(T, D), norm_gains, head_block, targets, rest_lse, cotangent)
    return grad_hidden.reshape(hidden.shape), grad_head, grad_gains


def solution(mesh):
    tokens = P(None, ("replica", "shard"))
    in_specs = (
        P(None, ("replica", "shard"), None),
        P(None, "shard"),
        P("shard", None),
        tokens,
        tokens,
        tokens,
    )
    out_specs = (P(None, ("replica", "shard"), None), P("shard", None), P(None, "shard"))
    return jax.shard_map(local, mesh=mesh, in_specs=in_specs, out_specs=out_specs, check_vma=False)
```

```python
import jax
import jax.numpy as jnp
from jax import lax
from jax.experimental import pallas as pl
from jax.experimental.pallas import tpu as pltpu
from jax.sharding import PartitionSpec as P

eps = 1e-06
F32, BF16, I32 = jnp.float32, jnp.bfloat16, jnp.int32
MESH = pl.DeviceIdType.MESH

D = 7168
HALF = D // 2
G = 896
W = 2 * G
GE = G + 128
V = 256
TK = 192
T = 2 * TK
RT = 32
NRT = T // RT
GN = 112
NSEM = 112


def iota(shape, dim):
    return lax.broadcasted_iota(I32, shape, dim)


def kernel(
    hid_ref, gain_ref, head_ref, tgt_ref, rest_ref, cot_ref,
    gx_ref, gw_ref, gg_ref,
    xv, nv, hv, r_own, r_sib, raw, gcol, gblk, gfull, scale_v,
    dl_t, dl_v, coef_v, dn_v, gacc, p_scr, xs, xr, sb, nq, tb, npb,
    zsum, zp, zr, yv, fr,
    local_sem, send_sem, recv_sem, zsend_sem, zrecv_sem, fsend_sem, frecv_sem, near_sem,
):
    zl = lax.axis_index("replica")
    shard = lax.axis_index("shard")
    c = shard & 1
    zh = (shard >> 1) & 1
    x = (shard >> 2) & 3
    y = shard >> 4
    z = zh * 4 + zl
    pc = x + c * (y - x)
    qc = y + c * (x - y)

    def device(q, p, zz, cc):
        xx = p + c * (q - p)
        yy = q + c * (p - q)
        return (zz & 3, ((yy * 4 + xx) * 2 + (zz >> 2)) * 2 + cc)

    def at(dq=0, dp=0):
        return device((qc + dq) & 3, (pc + dp) & 3, z, c)

    def up(dz, cc=c):
        return device(qc, pc, (z + dz) & 7, cc)

    sibling = (zl, shard + 1 - 2 * c)

    count = [0]
    started = []

    def send(src, dst, target, start=True):
        i = count[0]
        count[0] += 1
        copy = pltpu.make_async_remote_copy(
            src_ref=src, dst_ref=dst, send_sem=send_sem.at[i], recv_sem=recv_sem.at[i],
            device_id=target, device_id_type=MESH,
        )
        if start:
            copy.start()
            started.append(copy)
        return copy

    barrier = pltpu.get_barrier_semaphore()
    first = [sibling, at(dp=1), at(dp=-1), at(dq=1), at(dq=-1), up(1), up(-1), up(1, 1 - c), up(-1, 1 - c)]
    for partner in first:
        pl.semaphore_signal(barrier, inc=1, device_id=partner, device_id_type=MESH)

    loads = []
    for i in range(4):
        rows = pl.ds(i * 96, 96)
        copy = pltpu.make_async_copy(hid_ref.at[rows], xv.at[rows], local_sem.at[i])
        copy.start()
        loads.append(copy)

    w = zh * 2 + c
    hb = head_ref[...].astype(F32)
    for h in range(2):
        parts = [hb[:, (h * 4 + f) * G:(h * 4 + f + 1) * G] for f in range(4)]
        raw[h] = jnp.concatenate(parts, axis=0).astype(BF16)
    r_own[qc, pc, zh, c] = raw[c]
    gpad = jnp.concatenate([gain_ref[...].astype(F32), jnp.zeros((2, 128 - GN), F32)], axis=1)
    gcol[w] = jnp.concatenate([gpad, jnp.zeros((6, 128), F32)], axis=0)

    pl.semaphore_wait(barrier, len(first))

    def relay(i, targets):
        for target in targets:
            pl.semaphore_signal(near_sem.at[i], inc=1, device_id=target, device_id_type=MESH)

    relay(0, [at(dp=1), at(dp=-1), at(dq=1), at(dq=-1), up(1), up(-1)])

    edge = (zl == 0) | (zl == 3)
    step = jnp.where(zl == 3, 1, -1)
    m_h = send(raw.at[1 - c], r_own.at[pc, qc, zh, c], sibling)
    m_g = send(gcol.at[w], gcol.at[w], sibling)
    z_head = []
    for d in (1, 2):
        z_head.append([
            send(raw.at[c], r_own.at[qc, pc, zh, c], up(d * step), start=False),
            send(raw.at[1 - c], r_own.at[pc, qc, zh, c], up(d * step, 1 - c), start=False),
        ])

    @pl.when(edge)
    def _():
        for copy in z_head[0]:
            copy.start()

    pl.semaphore_wait(near_sem.at[0], 6)
    relay(1, [up(1), up(-1)])

    @pl.when(edge)
    def _():
        for copy in z_head[1]:
            copy.start()

    def z_arrives(near, far):
        @pl.when(edge)
        def _():
            for copy in near:
                copy.wait_recv()

        @pl.when(jnp.logical_not(edge))
        def _():
            for copy in far:
                copy.wait_recv()

    got = {}

    def along_q(k, dp):
        ref = r_own.at[qc, (pc + dp) & 3, k]
        for d in (1, 3, 2):
            got[k is zh, "q", dp, d] = send(ref, ref, at(dq=d))

    def begin(k):
        ref = r_own.at[qc, pc, k]
        for d in (1, 3, 2):
            got[k is zh, "p", d] = send(ref, ref, at(dp=d))
        along_q(k, 0)

    def p_arrives(k, d):
        got[k is zh, "p", d].wait_recv()
        along_q(k, -d)

    def to_sibling(k, q):
        ref = r_own.at[q & 3, :, k]
        got["sibling", count[0]] = send(ref, r_sib.at[q & 3, :, k], sibling)

    def q_arrives(k, d):
        for dp in (0, -1, -3, -2):
            got[k is zh, "q", dp, d].wait_recv()
        to_sibling(k, qc - d)

    def scale_tiles(begin_tile, end_tile):
        def body(i, carry):
            rows = pl.ds(pl.multiple_of(i * RT, RT), RT)
            total = jnp.zeros((RT, 128), F32)
            for j in range(D // G):
                part = xv[rows, j * G:(j + 1) * G].astype(F32)
                part = part * part
                for l in range(G // 128):
                    total += part[:, l * 128:(l + 1) * 128]
            mean = jnp.sum(total, axis=1, keepdims=True) * (1.0 / D)
            scale_v[rows] = jnp.broadcast_to(lax.rsqrt(mean + eps), (RT, 128))
            return carry
        lax.fori_loop(begin_tile, end_tile, body, 0)

    def lanes(v):
        return jnp.concatenate([v] * (G // 128), axis=1)

    def normed_tiles(begin_tile, end_tile):
        def body(i, carry):
            rows = pl.ds(pl.multiple_of(i * RT, RT), RT)
            k = jnp.where(i >= NRT // 2, 1, 0)
            s = lanes(scale_v[rows])
            for j in range(D // G):
                cols = slice(j * G, (j + 1) * G)
                g = gfull[k, :, cols]
                g = jnp.concatenate([g] * (RT // 8), axis=0)
                nv[rows, cols] = (xv[rows, cols].astype(F32) * s * g).astype(BF16)
            return carry
        lax.fori_loop(begin_tile, end_tile, body, 0)

    def spread_matrix():
        j = iota((128, G), 0)
        col = iota((128, G), 1)
        hit = jnp.zeros((128, G), jnp.bool_)
        for m in range(8):
            hit = hit | (col == j + GN * m)
        return jnp.where(hit & (j < GN), 1.0, 0.0).astype(BF16)

    def inside(rows, shift):
        r = iota((rows, G), 0)
        p = (r >> shift) & 3
        q = r >> (shift + 2)
        xx = p + c * (q - p)
        m = (xx & 1) * 4 + ((r >> 1) & 3)
        col = iota((rows, G), 1)
        return (col >= m * GN) & (col < (m + 1) * GN)

    def make_gains():
        lhs = gblk[...].reshape(128, 128).astype(BF16)
        u = jnp.dot(lhs, spread_matrix(), preferred_element_type=F32)
        u = jnp.where(inside(128, 3), u, 0.0).astype(BF16)
        o = iota((16, 128), 0)
        i = iota((16, 128), 1)
        p = (i >> 3) & 3
        q = i >> 5
        xx = p + c * (q - p)
        yy = q + c * (p - q)
        sel = ((yy * 2 + (xx >> 1)) == (o >> 1)) & ((i & 1) == (o & 1))
        full = jnp.dot(jnp.where(sel, 1.0, 0.0).astype(BF16), u, preferred_element_type=F32)
        for j in range(8):
            for k in range(2):
                row = full[2 * j + k:2 * j + k + 1]
                gfull[k, :, j * G:(j + 1) * G] = jnp.broadcast_to(row, (8, G))

    def permutation():
        o = iota((V, V), 0)
        i = iota((V, V), 1)
        src = ((o >> 4) & 3) * 64 + ((o >> 2) & 3) * 16 + (o >> 6) * 4 + (o & 3)
        return jnp.where(i == src, 1.0, 0.0).astype(BF16)

    def place(buf, half, core, q):
        q = q & 3
        rows = jnp.dot(permutation(), buf[q].reshape(V, G), preferred_element_type=F32).astype(BF16)
        for f in range(4):
            cols = pl.ds(pl.multiple_of(half * HALF + f * G, 128), G)
            for p in range(4):
                yy = q + core * (p - q)
                xx = p + core * (q - p)
                hv[yy * 4 + xx, :, cols] = rows[f * 64 + p * 16:f * 64 + (p + 1) * 16]

    other = 1 - zh
    m_h.wait_recv()
    begin(zh)
    m_g.wait_recv()
    pair = gcol.at[pl.ds(zh * 2, 2)]
    z_gain = [send(pair, pair, up(d * step), start=False) for d in (1, 2)]

    @pl.when(edge)
    def _():
        for copy in z_gain:
            copy.start()

    pl.semaphore_wait(near_sem.at[1], 2)
    relay(2, [up(1), up(-1)])
    loads[0].wait()
    scale_tiles(0, 3)
    for d in (1, 3, 2):
        p_arrives(zh, d)
    to_sibling(zh, qc)
    z_arrives(z_head[0], z_head[1])
    begin(other)
    z_arrives(z_gain[:1], z_gain[1:])
    gblk[qc, pc] = jnp.concatenate([gcol[i][0:2] for i in range(4)], axis=0)
    g_p = [send(gblk.at[qc, pc], gblk.at[qc, pc], at(dp=d)) for d in (1, 3, 2)]
    loads[1].wait()
    scale_tiles(3, 6)
    for d in (1, 3, 2):
        p_arrives(other, d)
    to_sibling(other, qc)
    for copy in g_p:
        copy.wait_recv()
    g_q = [send(gblk.at[qc], gblk.at[qc], at(dq=d)) for d in (1, 3, 2)]
    pl.semaphore_wait(near_sem.at[2], 2)
    loads[2].wait()
    loads[3].wait()
    scale_tiles(6, 12)
    for d in (1, 3, 2):
        q_arrives(zh, d)
    for copy in g_q:
        copy.wait_recv()
    make_gains()
    place(r_own, c, c, qc)
    normed_tiles(0, 6)
    q_arrives(other, 1)
    normed_tiles(6, 12)
    q_arrives(other, 3)
    place(r_own, c, c, qc - 1)
    place(r_own, c, c, qc - 3)
    q_arrives(other, 2)
    place(r_own, c, c, qc - 2)

    def logits_part(half, k):
        total = None
        for j in range(2):
            cols = pl.ds(pl.multiple_of(half * HALF + j * W, 128), W)
            part = lax.dot_general(
                hv[:, :, cols].reshape(V, W), nv[k * TK:(k + 1) * TK, cols],
                (((1,), (1,)), ((), ())), preferred_element_type=F32)
            total = part if total is None else total + part
        return total

    first_half = [logits_part(c, k) for k in range(2)]
    for key in list(got):
        if key[0] == "sibling":
            got[key].wait_recv()
    for q in range(4):
        place(r_sib, 1 - c, 1 - c, q)

    inner = []
    for k in range(2):
        logits = first_half[k] + logits_part(1 - c, k)
        total = jnp.log(jnp.exp(rest_ref[k:k + 1]) + jnp.sum(jnp.exp(logits), axis=0, keepdims=True))
        onehot = jnp.where(tgt_ref[k:k + 1] == iota((V, TK), 0), 1.0, 0.0)
        grad = (cot_ref[k:k + 1] * (jnp.exp(logits - total) - onehot)).astype(BF16)
        dl_t[k] = grad
        inner.append(jnp.sum(grad.astype(F32) * logits, axis=0, keepdims=True) * (1.0 / D))

    def partial(half, s):
        cols = pl.ds(pl.multiple_of(half * HALF + s * G, 128), G)
        for k in range(2):
            p_scr[k] = jnp.dot(
                dl_t[k], nv[k * TK:(k + 1) * TK, cols], preferred_element_type=F32).reshape(16, 16, G)
        return cols

    def fold(v):
        return v[0:8] + v[8:16]

    def give(s):
        cols = partial(1 - c, s)

        def body(b, acc):
            p0, p1 = p_scr[0, b], p_scr[1, b]
            xs[s, b] = (p0 + p1).astype(BF16)
            hf = hv[b, :, cols].astype(F32)
            return acc[0] + fold(hf * p0), acc[1] + fold(hf * p1)
        zero = jnp.zeros((8, G), F32)
        acc = lax.fori_loop(0, 16, body, (zero, zero))
        copy = send(xs.at[s], xr.at[s], sibling)
        for k in range(2):
            gacc[((1 - c) * 4 + s) * 2 + k] = acc[k] / gfull[k, :, cols]
        return copy

    def wide(s):
        return GE if s == 3 else G

    def take(s, copy):
        cols = partial(c, s)
        copy.wait_recv()

        def body(b, acc):
            p, q = b & 3, b >> 2
            yy = q + c * (p - q)
            xx = p + c * (q - p)
            e = yy * 4 + xx
            p0, p1 = p_scr[0, e], p_scr[1, e]
            sb[s, q, p, :, 0:G] = (p0 + p1 + xr[s, e].astype(F32)).astype(BF16)
            hf = hv[e, :, cols].astype(F32)
            return acc[0] + fold(hf * p0), acc[1] + fold(hf * p1)
        zero = jnp.zeros((8, G), F32)
        acc = lax.fori_loop(0, 16, body, (zero, zero))
        for k in range(2):
            gacc[(c * 4 + s) * 2 + k] = acc[k] / gfull[k, :, cols]
        if s == 3:
            rider()
        n = wide(s)
        for d in (2, 1, 3):
            got["rq", s, d] = send(
                sb.at[s, (qc + d) & 3, :, :, 0:n], nq.at[s, d - 1, :, :, 0:n], at(dq=d))

    def q_end(s):
        n = wide(s)
        for d in (1, 3, 2):
            got["rq", s, d].wait_recv()

        def body(p, carry):
            total = sb[s, qc, p, :, 0:n].astype(F32)
            for d in range(3):
                total = total + nq[s, d, p, :, 0:n].astype(F32)
            tb[s, p, :, 0:n] = total.astype(BF16)
            return carry
        lax.fori_loop(0, 4, body, 0)
        for d in (2, 1, 3):
            got["rp", s, d] = send(
                tb.at[s, (pc + d) & 3, :, 0:n], npb.at[s, d - 1, :, 0:n], at(dp=d))

    def p_end(s):
        n = wide(s)
        for d in (1, 3, 2):
            got["rp", s, d].wait_recv()
        total = tb[s, pc, :, 0:n].astype(F32)
        for d in range(3):
            total = total + npb[s, d, :, 0:n].astype(F32)
        zsum[s, :, 0:n] = total

    def z_copy(j, owner):
        n = G + 128 * j
        target = (owner >> 1) * 4 + (owner & 1) * 2 + j
        return pltpu.make_async_remote_copy(
            src_ref=zp.at[j, owner, :, 0:n], dst_ref=zr.at[z, :, 0:n],
            send_sem=zsend_sem.at[j, owner], recv_sem=zrecv_sem.at[z],
            device_id=device(qc, pc, target, c), device_id_type=MESH,
        )

    def z_begin(j):
        n = G + 128 * j
        for owner in range(4):
            rows = slice(owner * 4, owner * 4 + 4)
            zp[j, owner, :, 0:G] = jnp.concatenate(
                [zsum[2 * j, rows, 0:G], zsum[2 * j + 1, rows, 0:G]], axis=0)
            if j == 1:
                zp[j, owner, :, G:GE] = zsum[3, 0:8, G:GE]
        for owner in range(4):
            target = (owner >> 1) * 4 + (owner & 1) * 2 + j
            copy = z_copy(j, owner)

            @pl.when(target != z)
            def _():
                copy.start()

            @pl.when(target == z)
            def _():
                zr[z, :, 0:n] = zp[j, owner, :, 0:n]

    def f_copy(to):
        return pltpu.make_async_remote_copy(
            src_ref=yv, dst_ref=fr.at[c, zl & 1],
            send_sem=fsend_sem.at[to], recv_sem=frecv_sem.at[c * 2 + (zl & 1)],
            device_id=device(qc, pc, zh * 4 + to, zl >> 1), device_id_type=MESH,
        )

    def z_end(j):
        n = G + 128 * j

        @pl.when((zl & 1) == j)
        def _():
            for src in range(8):
                @pl.when(src != z)
                def _():
                    pltpu.make_async_remote_copy(
                        src_ref=zp.at[j, 0, :, 0:n], dst_ref=zr.at[src, :, 0:n],
                        send_sem=zsend_sem.at[j, 0], recv_sem=zrecv_sem.at[src],
                        device_id=sibling, device_id_type=MESH,
                    ).wait_recv()
            total = zr[0, :, 0:n]
            for src in range(1, 8):
                total = total + zr[src, :, 0:n]
            yv[:, 0:n] = total
            if j == 0:
                yv[:, G:GE] = jnp.zeros((8, 128), F32)
            for to in range(4):
                mine = (zl == to) & (c == (zl >> 1))

                @pl.when(jnp.logical_not(mine))
                def _():
                    f_copy(to).start()

                @pl.when(mine)
                def _():
                    fr[c, zl & 1] = yv[...]

    def hidden_block(j):
        cols = slice(j * G, (j + 1) * G)
        dn_v[...] = jnp.dot(dl_v[...], hv[:, :, cols].reshape(V, G), preferred_element_type=F32)
        for k in range(2):
            g = jnp.concatenate([gfull[k, :, cols]] * (RT // 8), axis=0)

            def body(i, carry):
                rows = pl.ds(pl.multiple_of(i * RT, RT), RT)
                gx_ref[rows, cols] = (
                    lanes(scale_v[rows]) * g * dn_v[rows]
                    - xv[rows, cols].astype(F32) * lanes(coef_v[rows])
                ).astype(BF16)
                return carry
            lax.fori_loop(k * NRT // 2, (k + 1) * NRT // 2, body, 0)

    def rider():
        full = jnp.concatenate(
            [jnp.sum(gacc[i], axis=0, keepdims=True) for i in range(16)], axis=0).astype(BF16)
        o = iota((V, 16), 0)
        i = iota((V, 16), 1)
        p = (o >> 4) & 3
        q = o >> 6
        xx = p + c * (q - p)
        yy = q + c * (p - q)
        sel = ((yy * 2 + (xx >> 1)) == (i >> 1)) & ((o & 1) == (i & 1)) & ((o & 15) < 8)
        u = jnp.dot(jnp.where(sel, 1.0, 0.0).astype(BF16), full, preferred_element_type=F32)
        u = jnp.where(inside(V, 4), u, 0.0).astype(BF16)
        out = lax.dot_general(
            u, spread_matrix(), (((1,), (1,)), ((), ())), preferred_element_type=F32)
        sb[3, :, :, :, G:GE] = out.astype(BF16).reshape(4, 4, 16, 128)

    x0 = give(0)
    x1 = give(1)
    take(0, x0)
    x2 = give(2)
    take(1, x1)
    x3 = give(3)
    take(2, x2)
    take(3, x3)
    for k in range(2):
        rows = slice(k * TK, (k + 1) * TK)
        dl_v[rows] = jnp.transpose(dl_t[k].astype(F32)).astype(BF16)
        sc = scale_v[rows]
        coef_v[rows] = jnp.transpose(jnp.broadcast_to(inner[k], (128, TK))) * sc * sc
    q_end(0)
    hidden_block(0)
    hidden_block(1)
    q_end(1)
    hidden_block(2)
    p_end(0)
    hidden_block(3)
    q_end(2)
    p_end(1)
    z_begin(0)
    hidden_block(4)
    q_end(3)
    p_end(2)
    hidden_block(5)
    z_end(0)
    p_end(3)
    z_begin(1)
    hidden_block(6)
    hidden_block(7)
    z_end(1)

    for src in range(2):
        for ch in range(2):
            mine = (c == src) & (zl == c * 2 + ch)

            @pl.when(jnp.logical_not(mine))
            def _():
                pltpu.make_async_remote_copy(
                    src_ref=yv, dst_ref=fr.at[src, ch],
                    send_sem=fsend_sem.at[0], recv_sem=frecv_sem.at[src * 2 + ch],
                    device_id=sibling, device_id_type=MESH,
                ).wait_recv()
            for sub in range(2):
                start = src * HALF + ch * W + sub * G
                gw_ref[:, start:start + G] = fr[src, ch, sub * 4:sub * 4 + 4, 0:G]
    gains = fr[0, 1, :, G:GE] + fr[1, 1, :, G:GE]
    mine = jnp.zeros((2, 128), F32)
    for i in range(4):
        mine = jnp.where(w == i, gains[i * 2:i * 2 + 2], mine)
    gg_ref[...] = mine[:, 0:GN]

    for copy in started:
        copy.wait_send()

    @pl.when(edge)
    def _():
        for copy in z_gain + z_head[0] + z_head[1]:
            copy.wait_send()
    for j in range(2):
        for owner in range(4):
            target = (owner >> 1) * 4 + (owner & 1) * 2 + j

            @pl.when(target != z)
            def _():
                z_copy(j, owner).wait_send()

    for to in range(4):
        @pl.when(jnp.logical_not((zl == to) & (c == (zl >> 1))))
        def _():
            f_copy(to).wait_send()


def local(hidden, norm_gains, head_block, targets, rest_lse, cotangent):
    any_space = pl.BlockSpec(memory_space=pl.ANY)
    vmem = pl.BlockSpec(memory_space=pltpu.VMEM)
    scratch = [
        pltpu.VMEM((T, D), BF16),
        pltpu.VMEM((T, D), BF16),
        pltpu.VMEM((16, 16, D), BF16),
        pltpu.VMEM((4, 4, 2, 2, 16, G), BF16),
        pltpu.VMEM((4, 4, 2, 2, 16, G), BF16),
        pltpu.VMEM((2, 16, G), BF16),
        pltpu.VMEM((4, 8, 128), F32),
        pltpu.VMEM((4, 4, 8, 128), F32),
        pltpu.VMEM((2, 8, D), F32),
        pltpu.VMEM((T, 128), F32),
        pltpu.VMEM((2, V, TK), BF16),
        pltpu.VMEM((T, V), BF16),
        pltpu.VMEM((T, 128), F32),
        pltpu.VMEM((T, G), F32),
        pltpu.VMEM((16, 8, G), F32),
        pltpu.VMEM((2, 16, 16, G), F32),
        pltpu.VMEM((4, 16, 16, G), BF16),
        pltpu.VMEM((4, 16, 16, G), BF16),
        pltpu.VMEM((4, 4, 4, 16, GE), BF16),
        pltpu.VMEM((4, 3, 4, 16, GE), BF16),
        pltpu.VMEM((4, 4, 16, GE), BF16),
        pltpu.VMEM((4, 3, 16, GE), BF16),
        pltpu.VMEM((4, 16, GE), F32),
        pltpu.VMEM((2, 4, 8, GE), F32),
        pltpu.VMEM((8, 8, GE), F32),
        pltpu.VMEM((8, GE), F32),
        pltpu.VMEM((2, 2, 8, GE), F32),
        pltpu.SemaphoreType.DMA((4,)),
        pltpu.SemaphoreType.DMA((NSEM,)),
        pltpu.SemaphoreType.DMA((NSEM,)),
        pltpu.SemaphoreType.DMA((2, 4)),
        pltpu.SemaphoreType.DMA((8,)),
        pltpu.SemaphoreType.DMA((4,)),
        pltpu.SemaphoreType.DMA((4,)),
        pltpu.SemaphoreType.REGULAR((3,)),
    ]
    grad_hidden, grad_head, grad_gains = pl.pallas_call(
        kernel,
        out_shape=(pltpu.VMEM((T, D), BF16), pltpu.VMEM((4, D), F32), pltpu.VMEM((2, GN), F32)),
        in_specs=[any_space, vmem, vmem, vmem, vmem, vmem],
        out_specs=(vmem, vmem, vmem),
        scratch_shapes=scratch,
        compiler_params=pltpu.CompilerParams(
            collective_id=0, has_side_effects=True, vmem_limit_bytes=50 << 20),
        cost_estimate=pl.CostEstimate(
            flops=6 * T * D * V, bytes_accessed=4 * T * D, transcendentals=2 * T * V),
        name="head_backward",
    )(hidden.reshape(T, D), norm_gains, head_block, targets, rest_lse, cotangent)
    return grad_hidden.reshape(hidden.shape), grad_head, grad_gains


def solution(mesh):
    tokens = P(None, ("replica", "shard"))
    in_specs = (
        P(None, ("replica", "shard"), None),
        P(None, "shard"),
        P("shard", None),
        tokens,
        tokens,
        tokens,
    )
    out_specs = (P(None, ("replica", "shard"), None), P("shard", None), P(None, "shard"))
    return jax.shard_map(local, mesh=mesh, in_specs=in_specs, out_specs=out_specs, check_vma=False)
```

```python
import jax
import jax.numpy as jnp
from jax import lax
from jax.experimental import pallas as pl
from jax.experimental.pallas import tpu as pltpu
from jax.sharding import PartitionSpec as P

eps = 1e-06
F32, BF16, I32 = jnp.float32, jnp.bfloat16, jnp.int32
MESH = pl.DeviceIdType.MESH

D = 7168
HALF = D // 2
G = 896
W = 2 * G
ZW = (G + 128) // 2
V = 256
TK = 192
T = 2 * TK
RT = 32
NRT = T // RT
GN = 112
NSEM = 112
SHARED = (0, 1, 2)


def iota(shape, dim):
    return lax.broadcasted_iota(I32, shape, dim)


def kernel(
    hid_ref, gain_ref, head_ref, tgt_ref, rest_ref, cot_ref,
    gx_ref, gw_ref, gg_ref,
    gain_v, head_v, tgt_v, rest_v, cot_v, xv, nv, hv, r_own, r_sib, raw, gcol, gblk, gfull, scale_v,
    dl_t, dl_v, coef_v, dn_v, gacc, gsb, gnq, gtb, gnp, gsum, xs, xr, sb, nq, zq, zf, nf, tb, npb,
    zsum, zp, zr, yv, fr,
    local_sem, send_sem, recv_sem, zsend_sem, zrecv_sem, fsend_sem, frecv_sem, near_sem,
):
    zl = lax.axis_index("replica")
    shard = lax.axis_index("shard")
    c = shard & 1
    zh = (shard >> 1) & 1
    x = (shard >> 2) & 3
    y = shard >> 4
    z = zh * 4 + zl
    pc = x + c * (y - x)
    qc = y + c * (x - y)

    def device(q, p, zz, cc):
        xx = p + c * (q - p)
        yy = q + c * (p - q)
        return (zz & 3, ((yy * 4 + xx) * 2 + (zz >> 2)) * 2 + cc)

    def at(dq=0, dp=0):
        return device((qc + dq) & 3, (pc + dp) & 3, z, c)

    def up(dz, cc=c):
        return device(qc, pc, (z + dz) & 7, cc)

    sibling = (zl, shard + 1 - 2 * c)

    count = [0]
    started = []

    def send(src, dst, target, start=True):
        i = count[0]
        count[0] += 1
        copy = pltpu.make_async_remote_copy(
            src_ref=src, dst_ref=dst, send_sem=send_sem.at[i], recv_sem=recv_sem.at[i],
            device_id=target, device_id_type=MESH,
        )
        if start:
            copy.start()
            started.append(copy)
        return copy

    barrier = pltpu.get_barrier_semaphore()
    first = [sibling, at(dp=1), at(dp=-1), at(dq=1), at(dq=-1)]
    for dz in (1, -1, 2, -2):
        first += [up(dz), up(dz, 1 - c)]
    for partner in first:
        pl.semaphore_signal(barrier, inc=1, device_id=partner, device_id_type=MESH)

    small_loads = []
    for i, (src, dst) in enumerate((
        (head_ref, head_v), (gain_ref, gain_v), (tgt_ref, tgt_v), (rest_ref, rest_v), (cot_ref, cot_v),
    )):
        copy = pltpu.make_async_copy(src, dst, local_sem.at[4 + i])
        copy.start()
        small_loads.append(copy)
    loads = []
    for i in range(4):
        rows = pl.ds(i * 96, 96)
        copy = pltpu.make_async_copy(hid_ref.at[rows], xv.at[rows], local_sem.at[i])
        copy.start()
        loads.append(copy)

    w = zh * 2 + c
    small_loads[0].wait()
    hb = head_v[...].astype(F32)
    for h in range(2):
        parts = [hb[:, (h * 4 + f) * G:(h * 4 + f + 1) * G] for f in range(4)]
        raw[h] = jnp.concatenate(parts, axis=0).astype(BF16)
    r_own[qc, pc, zh, c] = raw[c]
    small_loads[1].wait()
    gpad = jnp.concatenate([gain_v[...].astype(F32), jnp.zeros((2, 128 - GN), F32)], axis=1)
    gcol[w] = jnp.concatenate([gpad, jnp.zeros((6, 128), F32)], axis=0)

    pl.semaphore_wait(barrier, len(first))

    def relay(i, targets):
        for target in targets:
            pl.semaphore_signal(near_sem.at[i], inc=1, device_id=target, device_id_type=MESH)

    relay(0, [at(dp=1), at(dp=-1), at(dq=1), at(dq=-1), up(1), up(-1)])

    edge = (zl == 0) | (zl == 3)
    step = jnp.where(zl == 3, 1, -1)
    m_h = send(raw.at[1 - c], r_own.at[pc, qc, zh, c], sibling)
    m_g = send(gcol.at[w], gcol.at[w], sibling)
    z_head = []
    for d in (1, 2):
        z_head.append([
            send(raw.at[c], r_own.at[qc, pc, zh, c], up(d * step), start=False),
            send(raw.at[1 - c], r_own.at[pc, qc, zh, c], up(d * step, 1 - c), start=False),
        ])

    @pl.when(edge)
    def _():
        for copy in z_head[1] + z_head[0]:
            copy.start()

    def plane(d):
        return device(qc, pc, zh * 4 + ((zl + d) & 3), c)

    def far_begin():
        ref = r_own.at[qc, zl, zh]
        got["far"] = send(ref, ref, at(dq=2))

    def far_share():
        got["far"].wait_recv()
        ref = r_own.at[(qc - 2) & 3, zl, zh]
        for d in (1, 3, 2):
            got["share", d] = send(ref, ref, plane(d))

    def far_arrives():
        for d in (1, 3, 2):
            got["share", d].wait_recv()
        to_sibling(zh, 2)

    def z_arrives(near, far):
        @pl.when(edge)
        def _():
            for copy in near:
                copy.wait_recv()

        @pl.when(jnp.logical_not(edge))
        def _():
            for copy in far:
                copy.wait_recv()

    got = {}

    def along_q(k, dp):
        ref = r_own.at[qc, (pc + dp) & 3, k]
        for d in (1, 3) if k is zh else (1, 3, 2):
            got[k is zh, "q", dp, d] = send(ref, ref, at(dq=d))

    def begin(k):
        ref = r_own.at[qc, pc, k]
        for d in (1, 3, 2):
            got[k is zh, "p", d] = send(ref, ref, at(dp=d))

    def p_arrives(k, d):
        got[k is zh, "p", d].wait_recv()
        along_q(k, -d)

    def to_sibling(k, d):
        ref = r_own.at[(qc - d) & 3, :, k]
        got["sibling", d, k is zh] = send(ref, r_sib.at[(qc - d) & 3, :, k], sibling)

    def from_sibling(d):
        for key in list(got):
            if key[0] == "sibling" and key[1] == d:
                got[key].wait_recv()
        place(r_sib, 1 - c, 1 - c, pc - d)

    def q_arrives(k, d):
        for dp in (0, -1, -3, -2):
            got[k is zh, "q", dp, d].wait_recv()
            if d == 2:
                ref = r_own.at[(qc - d) & 3, (pc + dp) & 3, k]
                dst = r_sib.at[(qc - d) & 3, (pc + dp) & 3, k]
                got["sibling", d, k is zh, dp] = send(ref, dst, sibling)
        if d != 2:
            to_sibling(k, d)

    def scale_tiles(begin_tile, end_tile):
        def body(i, carry):
            rows = pl.ds(pl.multiple_of(i * RT, RT), RT)
            total = jnp.zeros((RT, 128), F32)
            for j in range(D // G):
                part = xv[rows, j * G:(j + 1) * G].astype(F32)
                part = part * part
                for l in range(G // 128):
                    total += part[:, l * 128:(l + 1) * 128]
            mean = jnp.sum(total, axis=1, keepdims=True) * (1.0 / D)
            scale_v[rows] = jnp.broadcast_to(lax.rsqrt(mean + eps), (RT, 128))
            return carry
        lax.fori_loop(begin_tile, end_tile, body, 0)

    def lanes(v):
        return jnp.concatenate([v] * (G // 128), axis=1)

    def normed_tiles(begin_tile, end_tile):
        def body(i, carry):
            rows = pl.ds(pl.multiple_of(i * RT, RT), RT)
            k = jnp.where(i >= NRT // 2, 1, 0)
            s = lanes(scale_v[rows])
            for j in range(D // G):
                cols = slice(j * G, (j + 1) * G)
                g = gfull[k, :, cols]
                g = jnp.concatenate([g] * (RT // 8), axis=0)
                nv[rows, cols] = (xv[rows, cols].astype(F32) * s * g).astype(BF16)
            return carry
        lax.fori_loop(begin_tile, end_tile, body, 0)

    def spread_matrix():
        j = iota((128, G), 0)
        col = iota((128, G), 1)
        hit = jnp.zeros((128, G), jnp.bool_)
        for m in range(8):
            hit = hit | (col == j + GN * m)
        return jnp.where(hit & (j < GN), 1.0, 0.0).astype(BF16)

    def inside(rows, shift):
        r = iota((rows, G), 0)
        p = (r >> shift) & 3
        q = r >> (shift + 2)
        xx = p + c * (q - p)
        m = (xx & 1) * 4 + ((r >> 1) & 3)
        col = iota((rows, G), 1)
        return (col >= m * GN) & (col < (m + 1) * GN)

    def make_gains():
        lhs = gblk[...].reshape(128, 128).astype(BF16)
        u = jnp.dot(lhs, spread_matrix(), preferred_element_type=F32)
        u = jnp.where(inside(128, 3), u, 0.0).astype(BF16)
        o = iota((16, 128), 0)
        i = iota((16, 128), 1)
        p = (i >> 3) & 3
        q = i >> 5
        xx = p + c * (q - p)
        yy = q + c * (p - q)
        sel = ((yy * 2 + (xx >> 1)) == (o >> 1)) & ((i & 1) == (o & 1))
        full = jnp.dot(jnp.where(sel, 1.0, 0.0).astype(BF16), u, preferred_element_type=F32)
        for j in range(8):
            for k in range(2):
                row = full[2 * j + k:2 * j + k + 1]
                gfull[k, :, j * G:(j + 1) * G] = jnp.broadcast_to(row, (8, G))

    def permutation():
        o = iota((V, V), 0)
        i = iota((V, V), 1)
        src = ((o >> 4) & 3) * 64 + ((o >> 2) & 3) * 16 + (o >> 6) * 4 + (o & 3)
        return jnp.where(i == src, 1.0, 0.0).astype(BF16)

    def place(buf, half, core, q):
        q = q & 3
        rows = jnp.dot(permutation(), buf[q].reshape(V, G), preferred_element_type=F32).astype(BF16)
        for f in range(4):
            cols = pl.ds(pl.multiple_of(half * HALF + f * G, 128), G)
            for p in range(4):
                yy = q + core * (p - q)
                xx = p + core * (q - p)
                hv[yy * 4 + xx, :, cols] = rows[f * 64 + p * 16:f * 64 + (p + 1) * 16]

    other = 1 - zh
    pl.semaphore_wait(near_sem.at[0], 6)
    relay(1, [up(1), up(-1)])
    m_h.wait_recv()
    begin(zh)
    along_q(zh, 0)
    m_g.wait_recv()
    pair = gcol.at[pl.ds(zh * 2, 2)]
    z_gain = [send(pair, pair, up(d * step), start=False) for d in (1, 2)]

    @pl.when(edge)
    def _():
        for copy in z_gain:
            copy.start()

    loads[0].wait()
    scale_tiles(0, 3)
    z_arrives(z_head[0], z_head[1])
    begin(other)
    for d in (1, 3, 2):
        p_arrives(zh, d)
    far_begin()
    along_q(other, 0)
    to_sibling(zh, 0)
    z_arrives(z_gain[:1], z_gain[1:])
    gblk[qc, pc] = jnp.concatenate([gcol[i][0:2] for i in range(4)], axis=0)
    g_p = [send(gblk.at[qc, pc], gblk.at[qc, pc], at(dp=d)) for d in (1, 3, 2)]
    loads[1].wait()
    scale_tiles(3, 6)
    for d in (1, 3, 2):
        p_arrives(other, d)
    to_sibling(other, 0)
    for copy in g_p:
        copy.wait_recv()
    g_q = [send(gblk.at[qc], gblk.at[qc], at(dq=d)) for d in (1, 3, 2)]
    pl.semaphore_wait(near_sem.at[1], 2)
    loads[2].wait()
    loads[3].wait()
    scale_tiles(6, 12)
    far_share()
    for d in (1, 3):
        q_arrives(zh, d)
    for copy in g_q:
        copy.wait_recv()
    make_gains()
    place(r_own, c, c, qc)
    from_sibling(0)
    normed_tiles(0, 4)
    far_arrives()
    normed_tiles(4, 8)
    q_arrives(other, 1)
    place(r_own, c, c, qc - 1)
    normed_tiles(8, 12)
    q_arrives(other, 3)
    place(r_own, c, c, qc - 3)
    from_sibling(1)
    q_arrives(other, 2)
    place(r_own, c, c, qc - 2)
    from_sibling(3)

    def logits_part(half, k):
        total = None
        for j in range(2):
            cols = pl.ds(pl.multiple_of(half * HALF + j * W, 128), W)
            part = lax.dot_general(
                hv[:, :, cols].reshape(V, W), nv[k * TK:(k + 1) * TK, cols],
                (((1,), (1,)), ((), ())), preferred_element_type=F32)
            total = part if total is None else total + part
        return total

    first_half = [logits_part(c, k) for k in range(2)]
    from_sibling(2)

    for copy in small_loads[2:]:
        copy.wait()
    inner = []
    for k in range(2):
        logits = first_half[k] + logits_part(1 - c, k)
        total = jnp.log(jnp.exp(rest_v[k:k + 1]) + jnp.sum(jnp.exp(logits), axis=0, keepdims=True))
        onehot = jnp.where(tgt_v[k:k + 1] == iota((V, TK), 0), 1.0, 0.0)
        grad = (cot_v[k:k + 1] * (jnp.exp(logits - total) - onehot)).astype(BF16)
        dl_t[k] = grad
        inner.append(jnp.sum(grad.astype(F32) * logits, axis=0, keepdims=True) * (1.0 / D))

    def partial(cols, k):
        return jnp.dot(dl_t[k], nv[k * TK:(k + 1) * TK, cols], preferred_element_type=F32)

    def block_cols(half, s):
        return pl.ds(pl.multiple_of(half * HALF + s * G, 128), G)

    def give(s):
        cols = block_cols(1 - c, s)
        xs[s] = (partial(cols, 0) + partial(cols, 1)).astype(BF16).reshape(16, 16, G)
        return send(xs.at[s], xr.at[s], sibling)

    def take(s, copy):
        cols = block_cols(c, s)
        own = partial(cols, 0) + partial(cols, 1)
        copy.wait_recv()
        for e in range(16):
            yy, xx = e >> 2, e & 3
            q, p = yy + c * (xx - yy), xx + c * (yy - xx)
            sb[s, q, p] = (own[e * 16:(e + 1) * 16] + xr[s, e].astype(F32)).astype(BF16)
        if s in SHARED:
            for d in (1, 3, 2):
                got["rz", s, d] = send(
                    sb.at[s, (qc + 2) & 3, (zl + d) & 3], zq.at[s, d - 1], plane(d))
        for d in (1, 3) if s in SHARED else (2, 1, 3):
            got["rq", s, d] = send(sb.at[s, (qc + d) & 3], nq.at[s, d - 1], at(dq=d))

    def far_sum(s):
        total = sb[s, (qc + 2) & 3, zl].astype(F32)
        for d in (1, 3, 2):
            got["rz", s, d].wait_recv()
            total = total + zq[s, d - 1].astype(F32)
        zf[s] = total.astype(BF16)
        got["rq", s, 2] = send(zf.at[s], nf.at[s], at(dq=2))

    def q_end(s):
        for d in (1, 3, 2):
            got["rq", s, d].wait_recv()
        for p in range(4):
            total = sb[s, qc, p].astype(F32)
            for d in (0, 2) if s in SHARED else range(3):
                total = total + nq[s, d, p].astype(F32)
            if s in SHARED:
                total = total + jnp.where(p == zl, nf[s].astype(F32), 0.0)
            tb[s, p] = total.astype(BF16)
        for d in (2, 1, 3):
            got["rp", s, d] = send(tb.at[s, (pc + d) & 3], npb.at[s, d - 1], at(dp=d))

    def p_end(s):
        for d in (1, 3, 2):
            got["rp", s, d].wait_recv()
        total = tb[s, pc].astype(F32)
        for d in range(3):
            total = total + npb[s, d].astype(F32)
        zsum[s] = total

    def gains_blocks():
        def body(j, carry):
            cols = pl.ds(pl.multiple_of(j * G, 128), G)
            hf = hv[:, :, cols].astype(F32).reshape(V // 8, 8, G)
            for k in range(2):
                part = partial(cols, k).reshape(V // 8, 8, G)
                gacc[j * 2 + k] = jnp.sum(hf * part, axis=0) / gfull[k, :, cols]
            return carry
        lax.fori_loop(0, 8, body, 0)

    def rider_begin():
        full = jnp.concatenate(
            [jnp.sum(gacc[i], axis=0, keepdims=True) for i in range(16)], axis=0).astype(BF16)
        o = iota((V, 16), 0)
        i = iota((V, 16), 1)
        p = (o >> 4) & 3
        q = o >> 6
        xx = p + c * (q - p)
        yy = q + c * (p - q)
        sel = ((yy * 2 + (xx >> 1)) == (i >> 1)) & ((o & 1) == (i & 1)) & ((o & 15) < 8)
        u = jnp.dot(jnp.where(sel, 1.0, 0.0).astype(BF16), full, preferred_element_type=F32)
        u = jnp.where(inside(V, 4), u, 0.0).astype(BF16)
        out = lax.dot_general(
            u, spread_matrix(), (((1,), (1,)), ((), ())), preferred_element_type=F32)
        gsb[...] = out.astype(BF16).reshape(4, 4, 16, 128)
        for d in (2, 1, 3):
            got["gq", d] = send(gsb.at[(qc + d) & 3], gnq.at[d - 1], at(dq=d))

    def rider_turn():
        for d in (1, 3, 2):
            got["gq", d].wait_recv()
        total = gsb[qc].astype(F32)
        for d in range(3):
            total = total + gnq[d].astype(F32)
        gtb[...] = total.astype(BF16)
        for d in (2, 1, 3):
            got["gp", d] = send(gtb.at[(pc + d) & 3], gnp.at[d - 1], at(dp=d))

    def rider_end():
        for d in (1, 3, 2):
            got["gp", d].wait_recv()
        total = gtb[pc].astype(F32)
        for d in range(3):
            total = total + gnp[d].astype(F32)
        gsum[...] = total

    def z_copy(j, owner):
        target = (owner >> 1) * 4 + (owner & 1) * 2 + j
        return pltpu.make_async_remote_copy(
            src_ref=zp.at[j, owner], dst_ref=zr.at[z],
            send_sem=zsend_sem.at[j, owner], recv_sem=zrecv_sem.at[z],
            device_id=device(qc, pc, target, c), device_id_type=MESH,
        )

    def z_begin(j):
        tail = gsum[0:8] if j == 1 else jnp.zeros((8, 128), F32)
        for owner in range(4):
            rows = slice(owner * 4, owner * 4 + 4)
            two = jnp.concatenate([zsum[2 * j, rows, 0:G], zsum[2 * j + 1, rows, 0:G]], axis=0)
            two = jnp.concatenate([two, tail], axis=1)
            zp[j, owner] = jnp.concatenate([two[:, 0:ZW], two[:, ZW:2 * ZW]], axis=0).astype(BF16)
        for owner in range(4):
            target = (owner >> 1) * 4 + (owner & 1) * 2 + j
            copy = z_copy(j, owner)

            @pl.when(target != z)
            def _():
                copy.start()

            @pl.when(target == z)
            def _():
                zr[z] = zp[j, owner]

    def f_copy(to):
        return pltpu.make_async_remote_copy(
            src_ref=yv, dst_ref=fr.at[c, zl & 1],
            send_sem=fsend_sem.at[to], recv_sem=frecv_sem.at[c * 2 + (zl & 1)],
            device_id=device(qc, pc, zh * 4 + to, zl >> 1), device_id_type=MESH,
        )

    def z_end(j):
        @pl.when((zl & 1) == j)
        def _():
            for src in range(8):
                @pl.when(src != z)
                def _():
                    pltpu.make_async_remote_copy(
                        src_ref=zp.at[j, 0], dst_ref=zr.at[src],
                        send_sem=zsend_sem.at[j, 0], recv_sem=zrecv_sem.at[src],
                        device_id=sibling, device_id_type=MESH,
                    ).wait_recv()
            total = zr[0].astype(F32)
            for src in range(1, 8):
                total = total + zr[src].astype(F32)
            yv[...] = total.astype(BF16)
            for to in (0, 3, 1, 2):
                mine = (zl == to) & (c == (zl >> 1))

                @pl.when(jnp.logical_not(mine))
                def _():
                    f_copy(to).start()

                @pl.when(mine)
                def _():
                    fr[c, zl & 1] = yv[...]

    def hidden_block(j):
        cols = slice(j * G, (j + 1) * G)
        dn_v[...] = jnp.dot(dl_v[...], hv[:, :, cols].reshape(V, G), preferred_element_type=F32)
        for k in range(2):
            g = jnp.concatenate([gfull[k, :, cols]] * (RT // 8), axis=0)

            def body(i, carry):
                rows = pl.ds(pl.multiple_of(i * RT, RT), RT)
                gx_ref[rows, cols] = (
                    lanes(scale_v[rows]) * g * dn_v[rows]
                    - xv[rows, cols].astype(F32) * lanes(coef_v[rows])
                ).astype(BF16)
                return carry
            lax.fori_loop(k * NRT // 2, (k + 1) * NRT // 2, body, 0)

    x0 = give(0)
    x1 = give(1)
    x2 = give(2)
    take(0, x0)
    x3 = give(3)
    take(1, x1)
    take(2, x2)
    take(3, x3)
    gains_blocks()
    rider_begin()
    for k in range(2):
        rows = slice(k * TK, (k + 1) * TK)
        dl_v[rows] = jnp.transpose(dl_t[k].astype(F32)).astype(BF16)
        sc = scale_v[rows]
        coef_v[rows] = jnp.transpose(jnp.broadcast_to(inner[k], (128, TK))) * sc * sc
    for i in SHARED:
        far_sum(i)
    hidden_block(0)
    hidden_block(1)
    q_end(0)
    rider_turn()
    hidden_block(2)
    q_end(1)
    hidden_block(3)
    q_end(2)
    p_end(0)
    q_end(3)
    p_end(1)
    z_begin(0)
    hidden_block(4)
    rider_end()
    p_end(2)
    hidden_block(5)
    p_end(3)
    z_begin(1)
    z_end(0)
    hidden_block(6)
    hidden_block(7)
    z_end(1)

    for src in range(2):
        for ch in range(2):
            mine = (c == src) & (zl == c * 2 + ch)

            @pl.when(jnp.logical_not(mine))
            def _():
                pltpu.make_async_remote_copy(
                    src_ref=yv, dst_ref=fr.at[src, ch],
                    send_sem=fsend_sem.at[0], recv_sem=frecv_sem.at[src * 2 + ch],
                    device_id=sibling, device_id_type=MESH,
                ).wait_recv()
            both = fr[src, ch].astype(F32)
            for sub in range(2):
                start = src * HALF + ch * W + sub * G
                gw_ref[:, start:start + ZW] = both[sub * 4:sub * 4 + 4]
                gw_ref[:, start + ZW:start + G] = both[8 + sub * 4:12 + sub * 4, 0:G - ZW]
    gains = fr[0, 1].astype(F32)[8:16, G - ZW:ZW] + fr[1, 1].astype(F32)[8:16, G - ZW:ZW]
    mine = jnp.zeros((2, 128), F32)
    for i in range(4):
        mine = jnp.where(w == i, gains[i * 2:i * 2 + 2], mine)
    gg_ref[...] = mine[:, 0:GN]

    for copy in started:
        copy.wait_send()

    @pl.when(edge)
    def _():
        for copy in z_gain + z_head[0] + z_head[1]:
            copy.wait_send()
    for j in range(2):
        for owner in range(4):
            target = (owner >> 1) * 4 + (owner & 1) * 2 + j

            @pl.when(target != z)
            def _():
                z_copy(j, owner).wait_send()

    for to in range(4):
        @pl.when(jnp.logical_not((zl == to) & (c == (zl >> 1))))
        def _():
            f_copy(to).wait_send()


def place_results(gx, gw, gg, gx_out, gw_out, gg_out, sem):
    copies = [
        pltpu.make_async_copy(gw, gw_out, sem.at[0]),
        pltpu.make_async_copy(gg, gg_out, sem.at[1]),
    ]
    for i in range(4):
        part = gx_out.at[i // 2, pl.ds(i % 2 * 96, 96)]
        copies.append(pltpu.make_async_copy(gx.at[i // 2, pl.ds(i % 2 * 96, 96)], part, sem.at[2 + i]))
    for copy in copies:
        copy.start()
    for copy in copies:
        copy.wait()


def local(hidden, norm_gains, head_block, targets, rest_lse, cotangent):
    any_space = pl.BlockSpec(memory_space=pl.ANY)
    vmem = pl.BlockSpec(memory_space=pltpu.VMEM)
    scratch = [
        pltpu.VMEM((2, GN), BF16),
        pltpu.VMEM((4, D), BF16),
        pltpu.VMEM((2, TK), I32),
        pltpu.VMEM((2, TK), F32),
        pltpu.VMEM((2, TK), F32),
        pltpu.VMEM((T, D), BF16),
        pltpu.VMEM((T, D), BF16),
        pltpu.VMEM((16, 16, D), BF16),
        pltpu.VMEM((4, 4, 2, 2, 16, G), BF16),
        pltpu.VMEM((4, 4, 2, 2, 16, G), BF16),
        pltpu.VMEM((2, 16, G), BF16),
        pltpu.VMEM((4, 8, 128), F32),
        pltpu.VMEM((4, 4, 8, 128), F32),
        pltpu.VMEM((2, 8, D), F32),
        pltpu.VMEM((T, 128), F32),
        pltpu.VMEM((2, V, TK), BF16),
        pltpu.VMEM((T, V), BF16),
        pltpu.VMEM((T, 128), F32),
        pltpu.VMEM((T, G), F32),
        pltpu.VMEM((16, 8, G), F32),
        pltpu.VMEM((4, 4, 16, 128), BF16),
        pltpu.VMEM((3, 4, 16, 128), BF16),
        pltpu.VMEM((4, 16, 128), BF16),
        pltpu.VMEM((3, 16, 128), BF16),
        pltpu.VMEM((16, 128), F32),
        pltpu.VMEM((4, 16, 16, G), BF16),
        pltpu.VMEM((4, 16, 16, G), BF16),
        pltpu.VMEM((4, 4, 4, 16, G), BF16),
        pltpu.VMEM((4, 3, 4, 16, G), BF16),
        pltpu.VMEM((3, 3, 16, G), BF16),
        pltpu.VMEM((3, 16, G), BF16),
        pltpu.VMEM((3, 16, G), BF16),
        pltpu.VMEM((4, 4, 16, G), BF16),
        pltpu.VMEM((4, 3, 16, G), BF16),
        pltpu.VMEM((4, 16, G), F32),
        pltpu.VMEM((2, 4, 16, ZW), BF16),
        pltpu.VMEM((8, 16, ZW), BF16),
        pltpu.VMEM((16, ZW), BF16),
        pltpu.VMEM((2, 2, 16, ZW), BF16),
        pltpu.SemaphoreType.DMA((9,)),
        pltpu.SemaphoreType.DMA((NSEM,)),
        pltpu.SemaphoreType.DMA((NSEM,)),
        pltpu.SemaphoreType.DMA((2, 4)),
        pltpu.SemaphoreType.DMA((8,)),
        pltpu.SemaphoreType.DMA((4,)),
        pltpu.SemaphoreType.DMA((4,)),
        pltpu.SemaphoreType.REGULAR((2,)),
    ]
    grad_hidden, grad_head, grad_gains = pl.pallas_call(
        kernel,
        out_shape=(pltpu.VMEM((T, D), BF16), pltpu.VMEM((4, D), F32), pltpu.VMEM((2, GN), F32)),
        in_specs=[any_space] * 6,
        out_specs=(vmem, vmem, vmem),
        scratch_shapes=scratch,
        compiler_params=pltpu.CompilerParams(
            collective_id=0, has_side_effects=True, vmem_limit_bytes=50 << 20),
        cost_estimate=pl.CostEstimate(
            flops=6 * T * D * V, bytes_accessed=4 * T * D, transcendentals=2 * T * V),
        name="head_backward",
    )(hidden.reshape(T, D), norm_gains, head_block, targets, rest_lse, cotangent)
    return pl.pallas_call(
        place_results,
        out_shape=(
            jax.ShapeDtypeStruct(hidden.shape, BF16),
            jax.ShapeDtypeStruct((4, D), F32),
            jax.ShapeDtypeStruct((2, GN), F32),
        ),
        in_specs=[vmem] * 3,
        out_specs=(any_space,) * 3,
        scratch_shapes=[pltpu.SemaphoreType.DMA((6,))],
        compiler_params=pltpu.CompilerParams(vmem_limit_bytes=16 << 20),
        name="place_results",
    )(*[pltpu.with_memory_space_constraint(v, pltpu.VMEM)
        for v in (grad_hidden.reshape(hidden.shape), grad_head, grad_gains)])


def solution(mesh):
    tokens = P(None, ("replica", "shard"))
    in_specs = (
        P(None, ("replica", "shard"), None),
        P(None, "shard"),
        P("shard", None),
        tokens,
        tokens,
        tokens,
    )
    out_specs = (P(None, ("replica", "shard"), None), P("shard", None), P(None, "shard"))
    return jax.shard_map(local, mesh=mesh, in_specs=in_specs, out_specs=out_specs, check_vma=False)
```

```python
import jax
import jax.numpy as jnp
from jax import lax
from jax.experimental import pallas as pl
from jax.experimental.pallas import tpu as pltpu
from jax.sharding import PartitionSpec as P

eps = 1e-06
F32, BF16, I32 = jnp.float32, jnp.bfloat16, jnp.int32
MESH = pl.DeviceIdType.MESH

D = 7168
HALF = D // 2
G = 896
W = 2 * G
ZW = (G + 128) // 2
V = 256
TK = 192
T = 2 * TK
RT = 32
NRT = T // RT
GN = 112
NSEM = 112
SHARED = (0, 1, 2)


def iota(shape, dim):
    return lax.broadcasted_iota(I32, shape, dim)


def kernel(
    hid_ref, gain_ref, head_ref, tgt_ref, rest_ref, cot_ref,
    gx_ref, gw_ref, gg_ref,
    gain_v, head_v, tgt_v, rest_v, cot_v, xv, nv, hv, r_own, r_sib, raw, gcol, gblk, gfull, scale_v,
    dl_t, dl_v, coef_v, dn_v, gacc, gsb, gnq, gtb, gnp, gsum, xs, xr, sb, nq, zq, zf, nf, tb, npb,
    zsum, zp, zr, yv, fr,
    local_sem, send_sem, recv_sem, zsend_sem, zrecv_sem, fsend_sem, frecv_sem, near_sem,
):
    zl = lax.axis_index("replica")
    shard = lax.axis_index("shard")
    c = shard & 1
    zh = (shard >> 1) & 1
    x = (shard >> 2) & 3
    y = shard >> 4
    z = zh * 4 + zl
    pc = x + c * (y - x)
    qc = y + c * (x - y)

    def device(q, p, zz, cc):
        xx = p + c * (q - p)
        yy = q + c * (p - q)
        return (zz & 3, ((yy * 4 + xx) * 2 + (zz >> 2)) * 2 + cc)

    def at(dq=0, dp=0):
        return device((qc + dq) & 3, (pc + dp) & 3, z, c)

    def up(dz, cc=c):
        return device(qc, pc, (z + dz) & 7, cc)

    sibling = (zl, shard + 1 - 2 * c)

    count = [0]
    started = []

    def send(src, dst, target, start=True):
        i = count[0]
        count[0] += 1
        copy = pltpu.make_async_remote_copy(
            src_ref=src, dst_ref=dst, send_sem=send_sem.at[i], recv_sem=recv_sem.at[i],
            device_id=target, device_id_type=MESH,
        )
        if start:
            copy.start()
            started.append(copy)
        return copy

    barrier = pltpu.get_barrier_semaphore()
    first = [sibling, at(dp=1), at(dp=-1), at(dq=1), at(dq=-1)]
    for dz in (1, -1, 2, -2):
        first += [up(dz), up(dz, 1 - c)]
    for partner in first:
        pl.semaphore_signal(barrier, inc=1, device_id=partner, device_id_type=MESH)

    small_loads = []
    for i, (src, dst) in enumerate((
        (head_ref, head_v), (gain_ref, gain_v), (tgt_ref, tgt_v), (rest_ref, rest_v), (cot_ref, cot_v),
    )):
        copy = pltpu.make_async_copy(src, dst, local_sem.at[4 + i])
        copy.start()
        small_loads.append(copy)
    loads = []
    for i in range(4):
        rows = pl.ds(i * 96, 96)
        copy = pltpu.make_async_copy(hid_ref.at[rows], xv.at[rows], local_sem.at[i])
        copy.start()
        loads.append(copy)

    w = zh * 2 + c
    small_loads[0].wait()
    hb = head_v[...].astype(F32)
    for h in range(2):
        parts = [hb[:, (h * 4 + f) * G:(h * 4 + f + 1) * G] for f in range(4)]
        raw[h] = jnp.concatenate(parts, axis=0).astype(BF16)
    r_own[qc, pc, zh, c] = raw[c]
    small_loads[1].wait()
    gpad = jnp.concatenate([gain_v[...].astype(F32), jnp.zeros((2, 128 - GN), F32)], axis=1)
    gcol[w] = jnp.concatenate([gpad, jnp.zeros((6, 128), F32)], axis=0)

    pl.semaphore_wait(barrier, len(first))

    def relay(i, targets):
        for target in targets:
            pl.semaphore_signal(near_sem.at[i], inc=1, device_id=target, device_id_type=MESH)

    relay(0, [at(dp=1), at(dp=-1), at(dq=1), at(dq=-1), up(1), up(-1)])

    edge = (zl == 0) | (zl == 3)
    step = jnp.where(zl == 3, 1, -1)
    m_h = send(raw.at[1 - c], r_own.at[pc, qc, zh, c], sibling)
    m_g = send(gcol.at[w], gcol.at[w], sibling)
    z_head = []
    for d in (1, 2):
        z_head.append([
            send(raw.at[c], r_own.at[qc, pc, zh, c], up(d * step), start=False),
            send(raw.at[1 - c], r_own.at[pc, qc, zh, c], up(d * step, 1 - c), start=False),
        ])

    @pl.when(edge)
    def _():
        for copy in z_head[1] + z_head[0]:
            copy.start()

    def plane(d):
        return device(qc, pc, zh * 4 + ((zl + d) & 3), c)

    def far_begin():
        ref = r_own.at[qc, zl, zh]
        got["far"] = send(ref, ref, at(dq=2))

    def far_share():
        got["far"].wait_recv()
        ref = r_own.at[(qc - 2) & 3, zl, zh]
        for d in (1, 3, 2):
            got["share", d] = send(ref, ref, plane(d))

    def far_arrives():
        for d in (1, 3, 2):
            got["share", d].wait_recv()
        to_sibling(zh, 2)

    def z_arrives(near, far):
        @pl.when(edge)
        def _():
            for copy in near:
                copy.wait_recv()

        @pl.when(jnp.logical_not(edge))
        def _():
            for copy in far:
                copy.wait_recv()

    got = {}

    def along_q(k, dp):
        ref = r_own.at[qc, (pc + dp) & 3, k]
        for d in (1, 3) if k is zh else (1, 3, 2):
            got[k is zh, "q", dp, d] = send(ref, ref, at(dq=d))

    def begin(k):
        ref = r_own.at[qc, pc, k]
        for d in (1, 3, 2):
            got[k is zh, "p", d] = send(ref, ref, at(dp=d))

    def p_arrives(k, d):
        got[k is zh, "p", d].wait_recv()
        if k is zh and d == 2:
            far_begin()
        along_q(k, -d)

    def to_sibling(k, d):
        ref = r_own.at[(qc - d) & 3, :, k]
        got["sibling", d, k is zh] = send(ref, r_sib.at[(qc - d) & 3, :, k], sibling)

    def from_sibling(d):
        for key in list(got):
            if key[0] == "sibling" and key[1] == d:
                got[key].wait_recv()
        place(r_sib, 1 - c, 1 - c, pc - d)

    def q_arrives(k, d):
        for dp in (0, -1, -3, -2):
            got[k is zh, "q", dp, d].wait_recv()
            if d == 2:
                ref = r_own.at[(qc - d) & 3, (pc + dp) & 3, k]
                dst = r_sib.at[(qc - d) & 3, (pc + dp) & 3, k]
                got["sibling", d, k is zh, dp] = send(ref, dst, sibling)
        if d != 2:
            to_sibling(k, d)

    def scale_tiles(begin_tile, end_tile):
        def body(i, carry):
            rows = pl.ds(pl.multiple_of(i * RT, RT), RT)
            total = jnp.zeros((RT, 128), F32)
            for j in range(D // G):
                part = xv[rows, j * G:(j + 1) * G].astype(F32)
                part = part * part
                for l in range(G // 128):
                    total += part[:, l * 128:(l + 1) * 128]
            mean = jnp.sum(total, axis=1, keepdims=True) * (1.0 / D)
            scale_v[rows] = jnp.broadcast_to(lax.rsqrt(mean + eps), (RT, 128))
            return carry
        lax.fori_loop(begin_tile, end_tile, body, 0)

    def lanes(v):
        return jnp.concatenate([v] * (G // 128), axis=1)

    def normed_tiles(begin_tile, end_tile):
        def body(i, carry):
            rows = pl.ds(pl.multiple_of(i * RT, RT), RT)
            k = jnp.where(i >= NRT // 2, 1, 0)
            s = lanes(scale_v[rows])
            for j in range(D // G):
                cols = slice(j * G, (j + 1) * G)
                g = gfull[k, :, cols]
                g = jnp.concatenate([g] * (RT // 8), axis=0)
                nv[rows, cols] = (xv[rows, cols].astype(F32) * s * g).astype(BF16)
            return carry
        lax.fori_loop(begin_tile, end_tile, body, 0)

    def spread_matrix():
        j = iota((128, G), 0)
        col = iota((128, G), 1)
        hit = jnp.zeros((128, G), jnp.bool_)
        for m in range(8):
            hit = hit | (col == j + GN * m)
        return jnp.where(hit & (j < GN), 1.0, 0.0).astype(BF16)

    def inside(rows, shift):
        r = iota((rows, G), 0)
        p = (r >> shift) & 3
        q = r >> (shift + 2)
        xx = p + c * (q - p)
        m = (xx & 1) * 4 + ((r >> 1) & 3)
        col = iota((rows, G), 1)
        return (col >= m * GN) & (col < (m + 1) * GN)

    def make_gains():
        lhs = gblk[...].reshape(128, 128).astype(BF16)
        u = jnp.dot(lhs, spread_matrix(), preferred_element_type=F32)
        u = jnp.where(inside(128, 3), u, 0.0).astype(BF16)
        o = iota((16, 128), 0)
        i = iota((16, 128), 1)
        p = (i >> 3) & 3
        q = i >> 5
        xx = p + c * (q - p)
        yy = q + c * (p - q)
        sel = ((yy * 2 + (xx >> 1)) == (o >> 1)) & ((i & 1) == (o & 1))
        full = jnp.dot(jnp.where(sel, 1.0, 0.0).astype(BF16), u, preferred_element_type=F32)
        for j in range(8):
            for k in range(2):
                row = full[2 * j + k:2 * j + k + 1]
                gfull[k, :, j * G:(j + 1) * G] = jnp.broadcast_to(row, (8, G))

    def permutation():
        o = iota((V, V), 0)
        i = iota((V, V), 1)
        src = ((o >> 4) & 3) * 64 + ((o >> 2) & 3) * 16 + (o >> 6) * 4 + (o & 3)
        return jnp.where(i == src, 1.0, 0.0).astype(BF16)

    def place(buf, half, core, q):
        q = q & 3
        rows = jnp.dot(permutation(), buf[q].reshape(V, G), preferred_element_type=F32).astype(BF16)
        for f in range(4):
            cols = pl.ds(pl.multiple_of(half * HALF + f * G, 128), G)
            for p in range(4):
                yy = q + core * (p - q)
                xx = p + core * (q - p)
                hv[yy * 4 + xx, :, cols] = rows[f * 64 + p * 16:f * 64 + (p + 1) * 16]

    other = 1 - zh
    pl.semaphore_wait(near_sem.at[0], 6)
    relay(1, [up(1), up(-1)])
    m_h.wait_recv()
    begin(zh)
    along_q(zh, 0)
    m_g.wait_recv()
    pair = gcol.at[pl.ds(zh * 2, 2)]
    z_gain = [send(pair, pair, up(d * step), start=False) for d in (1, 2)]

    @pl.when(edge)
    def _():
        for copy in z_gain:
            copy.start()

    loads[0].wait()
    scale_tiles(0, 3)
    z_arrives(z_head[0], z_head[1])
    begin(other)
    for d in (1, 3, 2):
        p_arrives(zh, d)
    along_q(other, 0)
    to_sibling(zh, 0)
    z_arrives(z_gain[:1], z_gain[1:])
    gblk[qc, pc] = jnp.concatenate([gcol[i][0:2] for i in range(4)], axis=0)
    g_p = [send(gblk.at[qc, pc], gblk.at[qc, pc], at(dp=d)) for d in (1, 3, 2)]
    loads[1].wait()
    scale_tiles(3, 6)
    for d in (1, 3, 2):
        p_arrives(other, d)
    to_sibling(other, 0)
    for copy in g_p:
        copy.wait_recv()
    g_q = [send(gblk.at[qc], gblk.at[qc], at(dq=d)) for d in (1, 3, 2)]
    pl.semaphore_wait(near_sem.at[1], 2)
    loads[2].wait()
    loads[3].wait()
    scale_tiles(6, 12)
    far_share()
    for d in (1, 3):
        q_arrives(zh, d)
    for copy in g_q:
        copy.wait_recv()
    make_gains()
    place(r_own, c, c, qc)
    from_sibling(0)
    normed_tiles(0, 4)
    far_arrives()
    normed_tiles(4, 8)
    q_arrives(other, 1)
    place(r_own, c, c, qc - 1)
    normed_tiles(8, 12)
    q_arrives(other, 3)
    place(r_own, c, c, qc - 3)
    from_sibling(1)
    q_arrives(other, 2)
    place(r_own, c, c, qc - 2)
    from_sibling(3)

    def logits_part(half, k):
        total = None
        for j in range(2):
            cols = pl.ds(pl.multiple_of(half * HALF + j * W, 128), W)
            part = lax.dot_general(
                hv[:, :, cols].reshape(V, W), nv[k * TK:(k + 1) * TK, cols],
                (((1,), (1,)), ((), ())), preferred_element_type=F32)
            total = part if total is None else total + part
        return total

    first_half = [logits_part(c, k) for k in range(2)]
    from_sibling(2)

    for copy in small_loads[2:]:
        copy.wait()
    inner = []
    for k in range(2):
        logits = first_half[k] + logits_part(1 - c, k)
        total = jnp.log(jnp.exp(rest_v[k:k + 1]) + jnp.sum(jnp.exp(logits), axis=0, keepdims=True))
        onehot = jnp.where(tgt_v[k:k + 1] == iota((V, TK), 0), 1.0, 0.0)
        grad = (cot_v[k:k + 1] * (jnp.exp(logits - total) - onehot)).astype(BF16)
        dl_t[k] = grad
        inner.append(jnp.sum(grad.astype(F32) * logits, axis=0, keepdims=True) * (1.0 / D))

    def partial(cols, k):
        return jnp.dot(dl_t[k], nv[k * TK:(k + 1) * TK, cols], preferred_element_type=F32)

    def block_cols(half, s):
        return pl.ds(pl.multiple_of(half * HALF + s * G, 128), G)

    def give(s):
        cols = block_cols(1 - c, s)
        xs[s] = (partial(cols, 0) + partial(cols, 1)).astype(BF16).reshape(16, 16, G)
        return send(xs.at[s], xr.at[s], sibling)

    def take(s, copy):
        cols = block_cols(c, s)
        own = partial(cols, 0) + partial(cols, 1)
        copy.wait_recv()
        for e in range(16):
            yy, xx = e >> 2, e & 3
            q, p = yy + c * (xx - yy), xx + c * (yy - xx)
            sb[s, q, p] = (own[e * 16:(e + 1) * 16] + xr[s, e].astype(F32)).astype(BF16)
        if s in SHARED:
            for d in (1, 3, 2):
                got["rz", s, d] = send(
                    sb.at[s, (qc + 2) & 3, (zl + d) & 3], zq.at[s, d - 1], plane(d))
        for d in (1, 3) if s in SHARED else (2, 1, 3):
            got["rq", s, d] = send(sb.at[s, (qc + d) & 3], nq.at[s, d - 1], at(dq=d))

    def far_sum(s):
        total = sb[s, (qc + 2) & 3, zl].astype(F32)
        for d in (1, 3, 2):
            got["rz", s, d].wait_recv()
            total = total + zq[s, d - 1].astype(F32)
        zf[s] = total.astype(BF16)
        got["rq", s, 2] = send(zf.at[s], nf.at[s], at(dq=2))

    def q_end(s):
        for d in (1, 3, 2):
            got["rq", s, d].wait_recv()
        for p in range(4):
            total = sb[s, qc, p].astype(F32)
            for d in (0, 2) if s in SHARED else range(3):
                total = total + nq[s, d, p].astype(F32)
            if s in SHARED:
                total = total + jnp.where(p == zl, nf[s].astype(F32), 0.0)
            tb[s, p] = total.astype(BF16)
        for d in (2, 1, 3):
            got["rp", s, d] = send(tb.at[s, (pc + d) & 3], npb.at[s, d - 1], at(dp=d))

    def p_end(s):
        for d in (1, 3, 2):
            got["rp", s, d].wait_recv()
        total = tb[s, pc].astype(F32)
        for d in range(3):
            total = total + npb[s, d].astype(F32)
        zsum[s] = total

    def gains_blocks():
        def body(j, carry):
            cols = pl.ds(pl.multiple_of(j * G, 128), G)
            hf = hv[:, :, cols].astype(F32).reshape(V // 8, 8, G)
            for k in range(2):
                part = partial(cols, k).reshape(V // 8, 8, G)
                gacc[j * 2 + k] = jnp.sum(hf * part, axis=0) / gfull[k, :, cols]
            return carry
        lax.fori_loop(0, 8, body, 0)

    def rider_begin():
        full = jnp.concatenate(
            [jnp.sum(gacc[i], axis=0, keepdims=True) for i in range(16)], axis=0).astype(BF16)
        o = iota((V, 16), 0)
        i = iota((V, 16), 1)
        p = (o >> 4) & 3
        q = o >> 6
        xx = p + c * (q - p)
        yy = q + c * (p - q)
        sel = ((yy * 2 + (xx >> 1)) == (i >> 1)) & ((o & 1) == (i & 1)) & ((o & 15) < 8)
        u = jnp.dot(jnp.where(sel, 1.0, 0.0).astype(BF16), full, preferred_element_type=F32)
        u = jnp.where(inside(V, 4), u, 0.0).astype(BF16)
        out = lax.dot_general(
            u, spread_matrix(), (((1,), (1,)), ((), ())), preferred_element_type=F32)
        gsb[...] = out.astype(BF16).reshape(4, 4, 16, 128)
        for d in (2, 1, 3):
            got["gq", d] = send(gsb.at[(qc + d) & 3], gnq.at[d - 1], at(dq=d))

    def rider_turn():
        for d in (1, 3, 2):
            got["gq", d].wait_recv()
        total = gsb[qc].astype(F32)
        for d in range(3):
            total = total + gnq[d].astype(F32)
        gtb[...] = total.astype(BF16)
        for d in (2, 1, 3):
            got["gp", d] = send(gtb.at[(pc + d) & 3], gnp.at[d - 1], at(dp=d))

    def rider_end():
        for d in (1, 3, 2):
            got["gp", d].wait_recv()
        total = gtb[pc].astype(F32)
        for d in range(3):
            total = total + gnp[d].astype(F32)
        gsum[...] = total

    def z_owner(j, owner):
        core = owner & 1
        return (owner >> 1) * 4 + (1 + core if j else 3 * core)

    mine_j = ((zl + 1) >> 1) & 1

    def z_copy(j, owner):
        target = z_owner(j, owner)
        return pltpu.make_async_remote_copy(
            src_ref=zp.at[j, owner], dst_ref=zr.at[z],
            send_sem=zsend_sem.at[j, owner], recv_sem=zrecv_sem.at[z],
            device_id=device(qc, pc, target, c), device_id_type=MESH,
        )

    def z_begin(j):
        tail = gsum[0:8] if j == 1 else jnp.zeros((8, 128), F32)
        for owner in range(4):
            rows = slice(owner * 4, owner * 4 + 4)
            two = jnp.concatenate([zsum[2 * j, rows, 0:G], zsum[2 * j + 1, rows, 0:G]], axis=0)
            two = jnp.concatenate([two, tail], axis=1)
            zp[j, owner] = jnp.concatenate([two[:, 0:ZW], two[:, ZW:2 * ZW]], axis=0).astype(BF16)
        for owner in range(4):
            target = z_owner(j, owner)
            copy = z_copy(j, owner)

            @pl.when(target != z)
            def _():
                copy.start()

            @pl.when(target == z)
            def _():
                zr[z] = zp[j, owner]

    def z_sent(j):
        for owner in range(4):
            @pl.when(z_owner(j, owner) != z)
            def _():
                z_copy(j, owner).wait_send()

    def f_copy(to):
        return pltpu.make_async_remote_copy(
            src_ref=yv, dst_ref=fr.at[c, mine_j],
            send_sem=fsend_sem.at[to], recv_sem=frecv_sem.at[c * 2 + mine_j],
            device_id=device(qc, pc, zh * 4 + to, zl >> 1), device_id_type=MESH,
        )

    def z_end(j):
        @pl.when(mine_j == j)
        def _():
            for src in range(8):
                @pl.when(src != z)
                def _():
                    pltpu.make_async_remote_copy(
                        src_ref=zp.at[j, 0], dst_ref=zr.at[src],
                        send_sem=zsend_sem.at[j, 0], recv_sem=zrecv_sem.at[src],
                        device_id=sibling, device_id_type=MESH,
                    ).wait_recv()
            total = zr[0].astype(F32)
            for src in range(1, 8):
                total = total + zr[src].astype(F32)
            yv[...] = total.astype(BF16)
            for to in (0, 3, 1, 2):
                mine = (zl == to) & (c == (zl >> 1))

                @pl.when(jnp.logical_not(mine))
                def _():
                    f_copy(to).start()

                @pl.when(mine)
                def _():
                    fr[c, mine_j] = yv[...]

    def hidden_block(j):
        cols = slice(j * G, (j + 1) * G)
        dn_v[...] = jnp.dot(dl_v[...], hv[:, :, cols].reshape(V, G), preferred_element_type=F32)
        for k in range(2):
            g = jnp.concatenate([gfull[k, :, cols]] * (RT // 8), axis=0)

            def body(i, carry):
                rows = pl.ds(pl.multiple_of(i * RT, RT), RT)
                gx_ref[rows, cols] = (
                    lanes(scale_v[rows]) * g * dn_v[rows]
                    - xv[rows, cols].astype(F32) * lanes(coef_v[rows])
                ).astype(BF16)
                return carry
            lax.fori_loop(k * NRT // 2, (k + 1) * NRT // 2, body, 0)

    x0 = give(0)
    x1 = give(1)
    x2 = give(2)
    take(0, x0)
    x3 = give(3)
    take(1, x1)
    take(2, x2)
    take(3, x3)
    gains_blocks()
    rider_begin()
    for k in range(2):
        rows = slice(k * TK, (k + 1) * TK)
        dl_v[rows] = jnp.transpose(dl_t[k].astype(F32)).astype(BF16)
        sc = scale_v[rows]
        coef_v[rows] = jnp.transpose(jnp.broadcast_to(inner[k], (128, TK))) * sc * sc
    for i in SHARED:
        far_sum(i)
    hidden_block(0)
    hidden_block(1)
    q_end(0)
    rider_turn()
    hidden_block(2)
    q_end(1)
    hidden_block(3)
    q_end(2)
    p_end(0)
    q_end(3)
    p_end(1)
    z_begin(0)
    hidden_block(4)
    rider_end()
    p_end(2)
    hidden_block(5)
    p_end(3)
    z_begin(1)
    z_end(0)
    hidden_block(6)
    hidden_block(7)
    for copy in started:
        copy.wait_send()
    started.clear()

    @pl.when(edge)
    def _():
        for copy in z_gain + z_head[0] + z_head[1]:
            copy.wait_send()
    z_sent(0)
    z_end(1)

    for src in range(2):
        for ch in range(2):
            mine = (c == src) & ((zl >> 1) == c) & (mine_j == ch)

            @pl.when(jnp.logical_not(mine))
            def _():
                pltpu.make_async_remote_copy(
                    src_ref=yv, dst_ref=fr.at[src, ch],
                    send_sem=fsend_sem.at[0], recv_sem=frecv_sem.at[src * 2 + ch],
                    device_id=sibling, device_id_type=MESH,
                ).wait_recv()
            both = fr[src, ch].astype(F32)
            for sub in range(2):
                start = src * HALF + ch * W + sub * G
                gw_ref[:, start:start + ZW] = both[sub * 4:sub * 4 + 4]
                gw_ref[:, start + ZW:start + G] = both[8 + sub * 4:12 + sub * 4, 0:G - ZW]
    gains = fr[0, 1].astype(F32)[8:16, G - ZW:ZW] + fr[1, 1].astype(F32)[8:16, G - ZW:ZW]
    mine = jnp.zeros((2, 128), F32)
    for i in range(4):
        mine = jnp.where(w == i, gains[i * 2:i * 2 + 2], mine)
    gg_ref[...] = mine[:, 0:GN]

    z_sent(1)
    for to in range(4):
        @pl.when(jnp.logical_not((zl == to) & (c == (zl >> 1))))
        def _():
            f_copy(to).wait_send()


def place_results(gx, gw, gg, gx_out, gw_out, gg_out, sem):
    copies = [
        pltpu.make_async_copy(gw, gw_out, sem.at[0]),
        pltpu.make_async_copy(gg, gg_out, sem.at[1]),
    ]
    for i in range(4):
        part = gx_out.at[i // 2, pl.ds(i % 2 * 96, 96)]
        copies.append(pltpu.make_async_copy(gx.at[i // 2, pl.ds(i % 2 * 96, 96)], part, sem.at[2 + i]))
    for copy in copies:
        copy.start()
    for copy in copies:
        copy.wait()


def local(hidden, norm_gains, head_block, targets, rest_lse, cotangent):
    any_space = pl.BlockSpec(memory_space=pl.ANY)
    vmem = pl.BlockSpec(memory_space=pltpu.VMEM)
    scratch = [
        pltpu.VMEM((2, GN), BF16),
        pltpu.VMEM((4, D), BF16),
        pltpu.VMEM((2, TK), I32),
        pltpu.VMEM((2, TK), F32),
        pltpu.VMEM((2, TK), F32),
        pltpu.VMEM((T, D), BF16),
        pltpu.VMEM((T, D), BF16),
        pltpu.VMEM((16, 16, D), BF16),
        pltpu.VMEM((4, 4, 2, 2, 16, G), BF16),
        pltpu.VMEM((4, 4, 2, 2, 16, G), BF16),
        pltpu.VMEM((2, 16, G), BF16),
        pltpu.VMEM((4, 8, 128), F32),
        pltpu.VMEM((4, 4, 8, 128), F32),
        pltpu.VMEM((2, 8, D), F32),
        pltpu.VMEM((T, 128), F32),
        pltpu.VMEM((2, V, TK), BF16),
        pltpu.VMEM((T, V), BF16),
        pltpu.VMEM((T, 128), F32),
        pltpu.VMEM((T, G), F32),
        pltpu.VMEM((16, 8, G), F32),
        pltpu.VMEM((4, 4, 16, 128), BF16),
        pltpu.VMEM((3, 4, 16, 128), BF16),
        pltpu.VMEM((4, 16, 128), BF16),
        pltpu.VMEM((3, 16, 128), BF16),
        pltpu.VMEM((16, 128), F32),
        pltpu.VMEM((4, 16, 16, G), BF16),
        pltpu.VMEM((4, 16, 16, G), BF16),
        pltpu.VMEM((4, 4, 4, 16, G), BF16),
        pltpu.VMEM((4, 3, 4, 16, G), BF16),
        pltpu.VMEM((3, 3, 16, G), BF16),
        pltpu.VMEM((3, 16, G), BF16),
        pltpu.VMEM((3, 16, G), BF16),
        pltpu.VMEM((4, 4, 16, G), BF16),
        pltpu.VMEM((4, 3, 16, G), BF16),
        pltpu.VMEM((4, 16, G), F32),
        pltpu.VMEM((2, 4, 16, ZW), BF16),
        pltpu.VMEM((8, 16, ZW), BF16),
        pltpu.VMEM((16, ZW), BF16),
        pltpu.VMEM((2, 2, 16, ZW), BF16),
        pltpu.SemaphoreType.DMA((9,)),
        pltpu.SemaphoreType.DMA((NSEM,)),
        pltpu.SemaphoreType.DMA((NSEM,)),
        pltpu.SemaphoreType.DMA((2, 4)),
        pltpu.SemaphoreType.DMA((8,)),
        pltpu.SemaphoreType.DMA((4,)),
        pltpu.SemaphoreType.DMA((4,)),
        pltpu.SemaphoreType.REGULAR((2,)),
    ]
    grad_hidden, grad_head, grad_gains = pl.pallas_call(
        kernel,
        out_shape=(pltpu.VMEM((T, D), BF16), pltpu.VMEM((4, D), F32), pltpu.VMEM((2, GN), F32)),
        in_specs=[any_space] * 6,
        out_specs=(vmem, vmem, vmem),
        scratch_shapes=scratch,
        compiler_params=pltpu.CompilerParams(
            collective_id=0, has_side_effects=True, vmem_limit_bytes=50 << 20),
        cost_estimate=pl.CostEstimate(
            flops=6 * T * D * V, bytes_accessed=4 * T * D, transcendentals=2 * T * V),
        name="head_backward",
    )(hidden.reshape(T, D), norm_gains, head_block, targets, rest_lse, cotangent)
    return pl.pallas_call(
        place_results,
        out_shape=(
            jax.ShapeDtypeStruct(hidden.shape, BF16),
            jax.ShapeDtypeStruct((4, D), F32),
            jax.ShapeDtypeStruct((2, GN), F32),
        ),
        in_specs=[vmem] * 3,
        out_specs=(any_space,) * 3,
        scratch_shapes=[pltpu.SemaphoreType.DMA((6,))],
        compiler_params=pltpu.CompilerParams(vmem_limit_bytes=16 << 20),
        name="place_results",
    )(*[pltpu.with_memory_space_constraint(v, pltpu.VMEM)
        for v in (grad_hidden.reshape(hidden.shape), grad_head, grad_gains)])


def solution(mesh):
    tokens = P(None, ("replica", "shard"))
    in_specs = (
        P(None, ("replica", "shard"), None),
        P(None, "shard"),
        P("shard", None),
        tokens,
        tokens,
        tokens,
    )
    out_specs = (P(None, ("replica", "shard"), None), P("shard", None), P(None, "shard"))
    return jax.shard_map(local, mesh=mesh, in_specs=in_specs, out_specs=out_specs, check_vma=False)
```

```python
import jax
import jax.numpy as jnp
from jax import lax
from jax.experimental import pallas as pl
from jax.experimental.pallas import tpu as pltpu
from jax.sharding import PartitionSpec as P

eps = 1e-06
F32, BF16, I32 = jnp.float32, jnp.bfloat16, jnp.int32
MESH = pl.DeviceIdType.MESH

D = 7168
HALF = D // 2
G = 896
W = 2 * G
ZW = (G + 128) // 2
V = 256
TK = 192
T = 2 * TK
RT = 32
NRT = T // RT
GN = 112
NSEM = 112
SHARED = (0, 1, 2)


def iota(shape, dim):
    return lax.broadcasted_iota(I32, shape, dim)


def kernel(
    hid_ref, gain_ref, head_ref, tgt_ref, rest_ref, cot_ref,
    gx_ref, gw_ref, gg_ref,
    gain_v, head_v, tgt_v, rest_v, cot_v, perm, xv, nv, hv, r_own, r_sib, raw, gcol, gblk, gfull, scale_v,
    dl_t, dl_v, coef_v, dn_v, gacc, gsb, gnq, gtb, gnp, gsum, xs, xr, sb, nq, zq, zf, nf, tb, npb,
    zsum, zp, zr, yv, fr,
    local_sem, send_sem, recv_sem, zsend_sem, zrecv_sem, fsend_sem, frecv_sem, near_sem,
):
    zl = lax.axis_index("replica")
    shard = lax.axis_index("shard")
    c = shard & 1
    zh = (shard >> 1) & 1
    x = (shard >> 2) & 3
    y = shard >> 4
    z = zh * 4 + zl
    pc = x + c * (y - x)
    qc = y + c * (x - y)

    def device(q, p, zz, cc):
        xx = p + c * (q - p)
        yy = q + c * (p - q)
        return (zz & 3, ((yy * 4 + xx) * 2 + (zz >> 2)) * 2 + cc)

    def at(dq=0, dp=0):
        return device((qc + dq) & 3, (pc + dp) & 3, z, c)

    def up(dz, cc=c):
        return device(qc, pc, (z + dz) & 7, cc)

    sibling = (zl, shard + 1 - 2 * c)

    count = [0]
    started = []

    def send(src, dst, target, start=True):
        i = count[0]
        count[0] += 1
        copy = pltpu.make_async_remote_copy(
            src_ref=src, dst_ref=dst, send_sem=send_sem.at[i], recv_sem=recv_sem.at[i],
            device_id=target, device_id_type=MESH,
        )
        if start:
            copy.start()
            started.append(copy)
        return copy

    barrier = pltpu.get_barrier_semaphore()
    first = [sibling, at(dp=1), at(dp=-1), at(dq=1), at(dq=-1)]
    for dz in (1, -1, 2, -2):
        first += [up(dz), up(dz, 1 - c)]
    for partner in first:
        pl.semaphore_signal(barrier, inc=1, device_id=partner, device_id_type=MESH)

    small_loads = []
    for i, (src, dst) in enumerate((
        (head_ref, head_v), (gain_ref, gain_v), (tgt_ref, tgt_v), (rest_ref, rest_v), (cot_ref, cot_v),
    )):
        copy = pltpu.make_async_copy(src, dst, local_sem.at[4 + i])
        copy.start()
        small_loads.append(copy)
    loads = []
    for i in range(4):
        rows = pl.ds(i * 96, 96)
        copy = pltpu.make_async_copy(hid_ref.at[rows], xv.at[rows], local_sem.at[i])
        copy.start()
        loads.append(copy)

    w = zh * 2 + c
    small_loads[0].wait()
    hb = head_v[...].astype(F32)
    for h in range(2):
        parts = [hb[:, (h * 4 + f) * G:(h * 4 + f + 1) * G] for f in range(4)]
        raw[h] = jnp.concatenate(parts, axis=0).astype(BF16)
    r_own[qc, pc, zh, c] = raw[c]
    small_loads[1].wait()
    gpad = jnp.concatenate([gain_v[...].astype(F32), jnp.zeros((2, 128 - GN), F32)], axis=1)
    gcol[w] = jnp.concatenate([gpad, jnp.zeros((6, 128), F32)], axis=0)

    pl.semaphore_wait(barrier, len(first))

    def relay(i, targets):
        for target in targets:
            pl.semaphore_signal(near_sem.at[i], inc=1, device_id=target, device_id_type=MESH)

    relay(0, [at(dp=1), at(dp=-1), at(dq=1), at(dq=-1), up(1), up(-1)])

    edge = (zl == 0) | (zl == 3)
    step = jnp.where(zl == 3, 1, -1)
    m_h = send(raw.at[1 - c], r_own.at[pc, qc, zh, c], sibling)
    m_g = send(gcol.at[w], gcol.at[w], sibling)
    z_head = []
    for d in (1, 2):
        z_head.append([
            send(raw.at[c], r_own.at[qc, pc, zh, c], up(d * step), start=False),
            send(raw.at[1 - c], r_own.at[pc, qc, zh, c], up(d * step, 1 - c), start=False),
        ])

    @pl.when(edge)
    def _():
        for copy in z_head[1] + z_head[0]:
            copy.start()

    def plane(d):
        return device(qc, pc, zh * 4 + ((zl + d) & 3), c)

    def far_begin():
        ref = r_own.at[qc, zl, zh]
        got["far"] = send(ref, ref, at(dq=2))

    def far_share():
        got["far"].wait_recv()
        ref = r_own.at[(qc - 2) & 3, zl, zh]
        for d in (1, 3, 2):
            got["share", d] = send(ref, ref, plane(d))

    def far_arrives():
        for d in (1, 3, 2):
            got["share", d].wait_recv()
        to_sibling(zh, 2)

    def z_arrives(near, far):
        @pl.when(edge)
        def _():
            for copy in near:
                copy.wait_recv()

        @pl.when(jnp.logical_not(edge))
        def _():
            for copy in far:
                copy.wait_recv()

    got = {}

    def along_q(k, dp):
        ref = r_own.at[qc, (pc + dp) & 3, k]
        for d in (1, 3) if k is zh else (1, 3, 2):
            got[k is zh, "q", dp, d] = send(ref, ref, at(dq=d))

    def begin(k):
        ref = r_own.at[qc, pc, k]
        for d in (1, 3, 2):
            got[k is zh, "p", d] = send(ref, ref, at(dp=d))

    def p_arrives(k, d):
        got[k is zh, "p", d].wait_recv()
        if k is zh and d == 2:
            far_begin()
        along_q(k, -d)

    def to_sibling(k, d):
        ref = r_own.at[(qc - d) & 3, :, k]
        got["sibling", d, k is zh] = send(ref, r_sib.at[(qc - d) & 3, :, k], sibling)

    def from_sibling(d):
        for key in list(got):
            if key[0] == "sibling" and key[1] == d:
                got[key].wait_recv()
        place(r_sib, 1 - c, 1 - c, pc - d)

    def q_arrives(k, d):
        for dp in (0, -1, -3, -2):
            got[k is zh, "q", dp, d].wait_recv()
            if d == 2:
                ref = r_own.at[(qc - d) & 3, (pc + dp) & 3, k]
                dst = r_sib.at[(qc - d) & 3, (pc + dp) & 3, k]
                got["sibling", d, k is zh, dp] = send(ref, dst, sibling)
        if d != 2:
            to_sibling(k, d)

    def scale_tiles(begin_tile, end_tile):
        def body(i, carry):
            rows = pl.ds(pl.multiple_of(i * RT, RT), RT)
            total = jnp.zeros((RT, 128), F32)
            for j in range(D // G):
                part = xv[rows, j * G:(j + 1) * G].astype(F32)
                part = part * part
                for l in range(G // 128):
                    total += part[:, l * 128:(l + 1) * 128]
            mean = jnp.sum(total, axis=1, keepdims=True) * (1.0 / D)
            scale_v[rows] = jnp.broadcast_to(lax.rsqrt(mean + eps), (RT, 128))
            return carry
        lax.fori_loop(begin_tile, end_tile, body, 0)

    def lanes(v):
        return jnp.concatenate([v] * (G // 128), axis=1)

    def normed_tiles(begin_tile, end_tile):
        def body(i, carry):
            rows = pl.ds(pl.multiple_of(i * RT, RT), RT)
            k = jnp.where(i >= NRT // 2, 1, 0)
            s = lanes(scale_v[rows])
            for j in range(D // G):
                cols = slice(j * G, (j + 1) * G)
                g = gfull[k, :, cols]
                g = jnp.concatenate([g] * (RT // 8), axis=0)
                nv[rows, cols] = (xv[rows, cols].astype(F32) * s * g).astype(BF16)
            return carry
        lax.fori_loop(begin_tile, end_tile, body, 0)

    def spread_matrix():
        j = iota((128, G), 0)
        col = iota((128, G), 1)
        hit = jnp.zeros((128, G), jnp.bool_)
        for m in range(8):
            hit = hit | (col == j + GN * m)
        return jnp.where(hit & (j < GN), 1.0, 0.0).astype(BF16)

    def inside(rows, shift):
        r = iota((rows, G), 0)
        p = (r >> shift) & 3
        q = r >> (shift + 2)
        xx = p + c * (q - p)
        m = (xx & 1) * 4 + ((r >> 1) & 3)
        col = iota((rows, G), 1)
        return (col >= m * GN) & (col < (m + 1) * GN)

    def make_gains():
        lhs = gblk[...].reshape(128, 128).astype(BF16)
        u = jnp.dot(lhs, spread_matrix(), preferred_element_type=F32)
        u = jnp.where(inside(128, 3), u, 0.0).astype(BF16)
        o = iota((16, 128), 0)
        i = iota((16, 128), 1)
        p = (i >> 3) & 3
        q = i >> 5
        xx = p + c * (q - p)
        yy = q + c * (p - q)
        sel = ((yy * 2 + (xx >> 1)) == (o >> 1)) & ((i & 1) == (o & 1))
        full = jnp.dot(jnp.where(sel, 1.0, 0.0).astype(BF16), u, preferred_element_type=F32)
        for j in range(8):
            for k in range(2):
                row = full[2 * j + k:2 * j + k + 1]
                gfull[k, :, j * G:(j + 1) * G] = jnp.broadcast_to(row, (8, G))

    def permutation():
        o = iota((V, V), 0)
        i = iota((V, V), 1)
        src = ((o >> 4) & 3) * 64 + ((o >> 2) & 3) * 16 + (o >> 6) * 4 + (o & 3)
        return jnp.where(i == src, 1.0, 0.0).astype(BF16)

    def place(buf, half, core, q):
        q = q & 3
        rows = jnp.dot(perm[...], buf[q].reshape(V, G), preferred_element_type=F32).astype(BF16)
        for f in range(4):
            cols = pl.ds(pl.multiple_of(half * HALF + f * G, 128), G)
            for p in range(4):
                yy = q + core * (p - q)
                xx = p + core * (q - p)
                hv[yy * 4 + xx, :, cols] = rows[f * 64 + p * 16:f * 64 + (p + 1) * 16]

    other = 1 - zh
    pl.semaphore_wait(near_sem.at[0], 6)
    relay(1, [up(1), up(-1)])
    m_h.wait_recv()
    begin(zh)
    along_q(zh, 0)
    m_g.wait_recv()
    pair = gcol.at[pl.ds(zh * 2, 2)]
    z_gain = [send(pair, pair, up(d * step), start=False) for d in (1, 2)]

    @pl.when(edge)
    def _():
        for copy in z_gain:
            copy.start()

    perm[...] = permutation()
    loads[0].wait()
    scale_tiles(0, 3)
    z_arrives(z_head[0], z_head[1])
    begin(other)
    for d in (1, 3, 2):
        p_arrives(zh, d)
    along_q(other, 0)
    to_sibling(zh, 0)
    z_arrives(z_gain[:1], z_gain[1:])
    gblk[qc, pc] = jnp.concatenate([gcol[i][0:2] for i in range(4)], axis=0)
    g_p = [send(gblk.at[qc, pc], gblk.at[qc, pc], at(dp=d)) for d in (1, 3, 2)]
    loads[1].wait()
    scale_tiles(3, 6)
    for d in (1, 3, 2):
        p_arrives(other, d)
    to_sibling(other, 0)
    for copy in g_p:
        copy.wait_recv()
    g_q = [send(gblk.at[qc], gblk.at[qc], at(dq=d)) for d in (1, 3, 2)]
    pl.semaphore_wait(near_sem.at[1], 2)
    loads[2].wait()
    loads[3].wait()
    scale_tiles(6, 12)
    far_share()
    for d in (1, 3):
        q_arrives(zh, d)
    for copy in g_q:
        copy.wait_recv()
    make_gains()
    place(r_own, c, c, qc)
    from_sibling(0)
    normed_tiles(0, 12)
    q_arrives(other, 1)
    q_arrives(other, 3)
    q_arrives(other, 2)
    far_arrives()
    place(r_own, c, c, qc - 1)
    place(r_own, c, c, qc - 3)
    place(r_own, c, c, qc - 2)
    from_sibling(1)
    from_sibling(3)

    def logits_part(half, k):
        total = None
        for j in range(2):
            cols = pl.ds(pl.multiple_of(half * HALF + j * W, 128), W)
            part = lax.dot_general(
                hv[:, :, cols].reshape(V, W), nv[k * TK:(k + 1) * TK, cols],
                (((1,), (1,)), ((), ())), preferred_element_type=F32)
            total = part if total is None else total + part
        return total

    first_half = [logits_part(c, k) for k in range(2)]
    from_sibling(2)

    for copy in small_loads[2:]:
        copy.wait()
    inner = []
    for k in range(2):
        logits = first_half[k] + logits_part(1 - c, k)
        total = jnp.log(jnp.exp(rest_v[k:k + 1]) + jnp.sum(jnp.exp(logits), axis=0, keepdims=True))
        onehot = jnp.where(tgt_v[k:k + 1] == iota((V, TK), 0), 1.0, 0.0)
        grad = (cot_v[k:k + 1] * (jnp.exp(logits - total) - onehot)).astype(BF16)
        dl_t[k] = grad
        inner.append(jnp.sum(grad.astype(F32) * logits, axis=0, keepdims=True) * (1.0 / D))

    def partial(cols, k):
        return jnp.dot(dl_t[k], nv[k * TK:(k + 1) * TK, cols], preferred_element_type=F32)

    def block_cols(half, s):
        return pl.ds(pl.multiple_of(half * HALF + s * G, 128), G)

    def give(s):
        cols = block_cols(1 - c, s)
        xs[s] = (partial(cols, 0) + partial(cols, 1)).astype(BF16).reshape(16, 16, G)
        return send(xs.at[s], xr.at[s], sibling)

    def take(s, copy):
        cols = block_cols(c, s)
        own = partial(cols, 0) + partial(cols, 1)
        copy.wait_recv()
        for e in range(16):
            yy, xx = e >> 2, e & 3
            q, p = yy + c * (xx - yy), xx + c * (yy - xx)
            sb[s, q, p] = (own[e * 16:(e + 1) * 16] + xr[s, e].astype(F32)).astype(BF16)
        if s in SHARED:
            for d in (1, 3, 2):
                got["rz", s, d] = send(
                    sb.at[s, (qc + 2) & 3, (zl + d) & 3], zq.at[s, d - 1], plane(d))
        for d in (1, 3) if s in SHARED else (2, 1, 3):
            got["rq", s, d] = send(sb.at[s, (qc + d) & 3], nq.at[s, d - 1], at(dq=d))

    def far_sum(s):
        total = sb[s, (qc + 2) & 3, zl].astype(F32)
        for d in (1, 3, 2):
            got["rz", s, d].wait_recv()
            total = total + zq[s, d - 1].astype(F32)
        zf[s] = total.astype(BF16)
        got["rq", s, 2] = send(zf.at[s], nf.at[s], at(dq=2))

    def q_end(s):
        for d in (1, 3, 2):
            got["rq", s, d].wait_recv()
        for p in range(4):
            total = sb[s, qc, p].astype(F32)
            for d in (0, 2) if s in SHARED else range(3):
                total = total + nq[s, d, p].astype(F32)
            if s in SHARED:
                total = total + jnp.where(p == zl, nf[s].astype(F32), 0.0)
            tb[s, p] = total.astype(BF16)
        for d in (2, 1, 3):
            got["rp", s, d] = send(tb.at[s, (pc + d) & 3], npb.at[s, d - 1], at(dp=d))

    def p_end(s):
        for d in (1, 3, 2):
            got["rp", s, d].wait_recv()
        total = tb[s, pc].astype(F32)
        for d in range(3):
            total = total + npb[s, d].astype(F32)
        zsum[s] = total

    def gains_blocks():
        def body(j, carry):
            cols = pl.ds(pl.multiple_of(j * G, 128), G)
            hf = hv[:, :, cols].astype(F32).reshape(V // 8, 8, G)
            for k in range(2):
                part = partial(cols, k).reshape(V // 8, 8, G)
                gacc[j * 2 + k] = jnp.sum(hf * part, axis=0) / gfull[k, :, cols]
            return carry
        lax.fori_loop(0, 8, body, 0)

    def rider_begin():
        full = jnp.concatenate(
            [jnp.sum(gacc[i], axis=0, keepdims=True) for i in range(16)], axis=0).astype(BF16)
        o = iota((V, 16), 0)
        i = iota((V, 16), 1)
        p = (o >> 4) & 3
        q = o >> 6
        xx = p + c * (q - p)
        yy = q + c * (p - q)
        sel = ((yy * 2 + (xx >> 1)) == (i >> 1)) & ((o & 1) == (i & 1)) & ((o & 15) < 8)
        u = jnp.dot(jnp.where(sel, 1.0, 0.0).astype(BF16), full, preferred_element_type=F32)
        u = jnp.where(inside(V, 4), u, 0.0).astype(BF16)
        out = lax.dot_general(
            u, spread_matrix(), (((1,), (1,)), ((), ())), preferred_element_type=F32)
        gsb[...] = out.astype(BF16).reshape(4, 4, 16, 128)
        for d in (2, 1, 3):
            got["gq", d] = send(gsb.at[(qc + d) & 3], gnq.at[d - 1], at(dq=d))

    def rider_turn():
        for d in (1, 3, 2):
            got["gq", d].wait_recv()
        total = gsb[qc].astype(F32)
        for d in range(3):
            total = total + gnq[d].astype(F32)
        gtb[...] = total.astype(BF16)
        for d in (2, 1, 3):
            got["gp", d] = send(gtb.at[(pc + d) & 3], gnp.at[d - 1], at(dp=d))

    def rider_end():
        for d in (1, 3, 2):
            got["gp", d].wait_recv()
        total = gtb[pc].astype(F32)
        for d in range(3):
            total = total + gnp[d].astype(F32)
        gsum[...] = total

    def z_owner(j, owner):
        core = owner & 1
        return (owner >> 1) * 4 + (1 + core if j else 3 * core)

    mine_j = ((zl + 1) >> 1) & 1

    def z_copy(j, owner):
        target = z_owner(j, owner)
        return pltpu.make_async_remote_copy(
            src_ref=zp.at[j, owner], dst_ref=zr.at[z],
            send_sem=zsend_sem.at[j, owner], recv_sem=zrecv_sem.at[z],
            device_id=device(qc, pc, target, c), device_id_type=MESH,
        )

    def z_begin(j):
        tail = gsum[0:8] if j == 1 else jnp.zeros((8, 128), F32)
        for owner in range(4):
            rows = slice(owner * 4, owner * 4 + 4)
            two = jnp.concatenate([zsum[2 * j, rows, 0:G], zsum[2 * j + 1, rows, 0:G]], axis=0)
            two = jnp.concatenate([two, tail], axis=1)
            zp[j, owner] = jnp.concatenate([two[:, 0:ZW], two[:, ZW:2 * ZW]], axis=0).astype(BF16)
        for owner in range(4):
            target = z_owner(j, owner)
            copy = z_copy(j, owner)

            @pl.when(target != z)
            def _():
                copy.start()

            @pl.when(target == z)
            def _():
                zr[z] = zp[j, owner]

    def z_sent(j):
        for owner in range(4):
            @pl.when(z_owner(j, owner) != z)
            def _():
                z_copy(j, owner).wait_send()

    def f_copy(to):
        return pltpu.make_async_remote_copy(
            src_ref=yv, dst_ref=fr.at[c, mine_j],
            send_sem=fsend_sem.at[to], recv_sem=frecv_sem.at[c * 2 + mine_j],
            device_id=device(qc, pc, zh * 4 + to, zl >> 1), device_id_type=MESH,
        )

    def z_end(j):
        @pl.when(mine_j == j)
        def _():
            for src in range(8):
                @pl.when(src != z)
                def _():
                    pltpu.make_async_remote_copy(
                        src_ref=zp.at[j, 0], dst_ref=zr.at[src],
                        send_sem=zsend_sem.at[j, 0], recv_sem=zrecv_sem.at[src],
                        device_id=sibling, device_id_type=MESH,
                    ).wait_recv()
            total = zr[0].astype(F32)
            for src in range(1, 8):
                total = total + zr[src].astype(F32)
            yv[...] = total.astype(BF16)
            for to in (0, 3, 1, 2):
                mine = (zl == to) & (c == (zl >> 1))

                @pl.when(jnp.logical_not(mine))
                def _():
                    f_copy(to).start()

                @pl.when(mine)
                def _():
                    fr[c, mine_j] = yv[...]

    def hidden_block(j):
        cols = slice(j * G, (j + 1) * G)
        dn_v[...] = jnp.dot(dl_v[...], hv[:, :, cols].reshape(V, G), preferred_element_type=F32)
        for k in range(2):
            g = jnp.concatenate([gfull[k, :, cols]] * (RT // 8), axis=0)

            def body(i, carry):
                rows = pl.ds(pl.multiple_of(i * RT, RT), RT)
                gx_ref[rows, cols] = (
                    lanes(scale_v[rows]) * g * dn_v[rows]
                    - xv[rows, cols].astype(F32) * lanes(coef_v[rows])
                ).astype(BF16)
                return carry
            lax.fori_loop(k * NRT // 2, (k + 1) * NRT // 2, body, 0)

    x0 = give(0)
    x1 = give(1)
    x2 = give(2)
    take(0, x0)
    x3 = give(3)
    take(1, x1)
    take(2, x2)
    take(3, x3)
    gains_blocks()
    rider_begin()
    for k in range(2):
        rows = slice(k * TK, (k + 1) * TK)
        dl_v[rows] = jnp.transpose(dl_t[k].astype(F32)).astype(BF16)
        sc = scale_v[rows]
        coef_v[rows] = jnp.transpose(jnp.broadcast_to(inner[k], (128, TK))) * sc * sc
    for i in SHARED:
        far_sum(i)
    hidden_block(0)
    hidden_block(1)
    q_end(0)
    rider_turn()
    hidden_block(2)
    q_end(1)
    hidden_block(3)
    q_end(2)
    p_end(0)
    q_end(3)
    p_end(1)
    z_begin(0)
    hidden_block(4)
    rider_end()
    p_end(2)
    hidden_block(5)
    p_end(3)
    z_begin(1)
    z_end(0)
    hidden_block(6)
    hidden_block(7)
    for copy in started:
        copy.wait_send()
    started.clear()

    @pl.when(edge)
    def _():
        for copy in z_gain + z_head[0] + z_head[1]:
            copy.wait_send()
    z_sent(0)
    z_end(1)

    for src in range(2):
        for ch in range(2):
            mine = (c == src) & ((zl >> 1) == c) & (mine_j == ch)

            @pl.when(jnp.logical_not(mine))
            def _():
                pltpu.make_async_remote_copy(
                    src_ref=yv, dst_ref=fr.at[src, ch],
                    send_sem=fsend_sem.at[0], recv_sem=frecv_sem.at[src * 2 + ch],
                    device_id=sibling, device_id_type=MESH,
                ).wait_recv()
            both = fr[src, ch].astype(F32)
            for sub in range(2):
                start = src * HALF + ch * W + sub * G
                gw_ref[:, start:start + ZW] = both[sub * 4:sub * 4 + 4]
                gw_ref[:, start + ZW:start + G] = both[8 + sub * 4:12 + sub * 4, 0:G - ZW]
    gains = fr[0, 1].astype(F32)[8:16, G - ZW:ZW] + fr[1, 1].astype(F32)[8:16, G - ZW:ZW]
    mine = jnp.zeros((2, 128), F32)
    for i in range(4):
        mine = jnp.where(w == i, gains[i * 2:i * 2 + 2], mine)
    gg_ref[...] = mine[:, 0:GN]

    z_sent(1)
    for to in range(4):
        @pl.when(jnp.logical_not((zl == to) & (c == (zl >> 1))))
        def _():
            f_copy(to).wait_send()


def place_results(gx, gw, gg, gx_out, gw_out, gg_out, sem):
    copies = [
        pltpu.make_async_copy(gw, gw_out, sem.at[0]),
        pltpu.make_async_copy(gg, gg_out, sem.at[1]),
    ]
    for i in range(4):
        part = gx_out.at[i // 2, pl.ds(i % 2 * 96, 96)]
        copies.append(pltpu.make_async_copy(gx.at[i // 2, pl.ds(i % 2 * 96, 96)], part, sem.at[2 + i]))
    for copy in copies:
        copy.start()
    for copy in copies:
        copy.wait()


def local(hidden, norm_gains, head_block, targets, rest_lse, cotangent):
    any_space = pl.BlockSpec(memory_space=pl.ANY)
    vmem = pl.BlockSpec(memory_space=pltpu.VMEM)
    scratch = [
        pltpu.VMEM((2, GN), BF16),
        pltpu.VMEM((4, D), BF16),
        pltpu.VMEM((2, TK), I32),
        pltpu.VMEM((2, TK), F32),
        pltpu.VMEM((2, TK), F32),
        pltpu.VMEM((V, V), BF16),
        pltpu.VMEM((T, D), BF16),
        pltpu.VMEM((T, D), BF16),
        pltpu.VMEM((16, 16, D), BF16),
        pltpu.VMEM((4, 4, 2, 2, 16, G), BF16),
        pltpu.VMEM((4, 4, 2, 2, 16, G), BF16),
        pltpu.VMEM((2, 16, G), BF16),
        pltpu.VMEM((4, 8, 128), F32),
        pltpu.VMEM((4, 4, 8, 128), F32),
        pltpu.VMEM((2, 8, D), F32),
        pltpu.VMEM((T, 128), F32),
        pltpu.VMEM((2, V, TK), BF16),
        pltpu.VMEM((T, V), BF16),
        pltpu.VMEM((T, 128), F32),
        pltpu.VMEM((T, G), F32),
        pltpu.VMEM((16, 8, G), F32),
        pltpu.VMEM((4, 4, 16, 128), BF16),
        pltpu.VMEM((3, 4, 16, 128), BF16),
        pltpu.VMEM((4, 16, 128), BF16),
        pltpu.VMEM((3, 16, 128), BF16),
        pltpu.VMEM((16, 128), F32),
        pltpu.VMEM((4, 16, 16, G), BF16),
        pltpu.VMEM((4, 16, 16, G), BF16),
        pltpu.VMEM((4, 4, 4, 16, G), BF16),
        pltpu.VMEM((4, 3, 4, 16, G), BF16),
        pltpu.VMEM((3, 3, 16, G), BF16),
        pltpu.VMEM((3, 16, G), BF16),
        pltpu.VMEM((3, 16, G), BF16),
        pltpu.VMEM((4, 4, 16, G), BF16),
        pltpu.VMEM((4, 3, 16, G), BF16),
        pltpu.VMEM((4, 16, G), F32),
        pltpu.VMEM((2, 4, 16, ZW), BF16),
        pltpu.VMEM((8, 16, ZW), BF16),
        pltpu.VMEM((16, ZW), BF16),
        pltpu.VMEM((2, 2, 16, ZW), BF16),
        pltpu.SemaphoreType.DMA((9,)),
        pltpu.SemaphoreType.DMA((NSEM,)),
        pltpu.SemaphoreType.DMA((NSEM,)),
        pltpu.SemaphoreType.DMA((2, 4)),
        pltpu.SemaphoreType.DMA((8,)),
        pltpu.SemaphoreType.DMA((4,)),
        pltpu.SemaphoreType.DMA((4,)),
        pltpu.SemaphoreType.REGULAR((2,)),
    ]
    grad_hidden, grad_head, grad_gains = pl.pallas_call(
        kernel,
        out_shape=(pltpu.VMEM((T, D), BF16), pltpu.VMEM((4, D), F32), pltpu.VMEM((2, GN), F32)),
        in_specs=[any_space] * 6,
        out_specs=(vmem, vmem, vmem),
        scratch_shapes=scratch,
        compiler_params=pltpu.CompilerParams(
            collective_id=0, has_side_effects=True, vmem_limit_bytes=50 << 20),
        cost_estimate=pl.CostEstimate(
            flops=6 * T * D * V, bytes_accessed=4 * T * D, transcendentals=2 * T * V),
        name="head_backward",
    )(hidden.reshape(T, D), norm_gains, head_block, targets, rest_lse, cotangent)
    return pl.pallas_call(
        place_results,
        out_shape=(
            jax.ShapeDtypeStruct(hidden.shape, BF16),
            jax.ShapeDtypeStruct((4, D), F32),
            jax.ShapeDtypeStruct((2, GN), F32),
        ),
        in_specs=[vmem] * 3,
        out_specs=(any_space,) * 3,
        scratch_shapes=[pltpu.SemaphoreType.DMA((6,))],
        compiler_params=pltpu.CompilerParams(vmem_limit_bytes=16 << 20),
        name="place_results",
    )(*[pltpu.with_memory_space_constraint(v, pltpu.VMEM)
        for v in (grad_hidden.reshape(hidden.shape), grad_head, grad_gains)])


def solution(mesh):
    tokens = P(None, ("replica", "shard"))
    in_specs = (
        P(None, ("replica", "shard"), None),
        P(None, "shard"),
        P("shard", None),
        tokens,
        tokens,
        tokens,
    )
    out_specs = (P(None, ("replica", "shard"), None), P("shard", None), P(None, "shard"))
    return jax.shard_map(local, mesh=mesh, in_specs=in_specs, out_specs=out_specs, check_vma=False)
```
